32 devices in a mesh: img: 16 (over z, y, core), ch: 2 (over x).
Axes of the slice: x: 2, y: 2, z: 4, core: 2. Of those that a mesh axis runs over, the one named last changes fastest.
Arguments:
- features: bfloat16 [512, 64, 1024], P('ch', 'img'), may hold values from -6 to 6
- latents: bfloat16 [64, 512], P('img'), may hold values from -6 to 6
- skip_rgb: float32 [3, 64, 1024], P(None, 'img'), may hold values from -6 to 6
- noises: float32 [2, 64, 4096], P(None, 'img'), may hold values from -6 to 6
- ada_shift: int32 [64, 2], P('img'), may hold values from -8 to 8
- crop_mask: int32 [64, 4096], P('img'), may hold values 0 or 1
- critic_mix: float32 [64, 3], replicated, may hold values from -3.5 to 3.5
- critic_bias: float32 [64], replicated, may hold values from -3 to 3
- critic_out: float32 [64], replicated, may hold values from -0.75 to 0.75
- upsampler: float32 [512, 9, 512], P('ch', None, 'img'), may hold values from -6 to 6
- upsampler_mean: float32 [512, 9, 512], P('ch', None, 'img'), may hold values from -0.0222 to 0.0222
- upsampler_square: float32 [512, 9, 512], P('ch', None, 'img'), may hold values from 2.525e-05 to 0.000101
- refiner: float32 [512, 9, 512], P('ch', None, 'img'), may hold values from -6 to 6
- refiner_mean: float32 [512, 9, 512], P('ch', None, 'img'), may hold values from -5.0835886 to 5.0835886
- refiner_square: float32 [512, 9, 512], P('ch', None, 'img'), may hold values from 1.3240252 to 5.2961006
- affines: float32 [3, 512, 512], P(None, 'img', 'ch'), may hold values from -6 to 6
- affines_mean: float32 [3, 512, 512], P(None, 'img', 'ch'), may hold values from -2.845607 to 2.845607
- affines_square: float32 [3, 512, 512], P(None, 'img', 'ch'), may hold values from 0.41486356 to 1.6594542
- modbias: float32 [3, 512], P(None, 'ch'), may hold values from 0.5 to 1.5
- modbias_mean: float32 [3, 512], P(None, 'ch'), may hold values from -514.3959 to 514.3959
- modbias_square: float32 [3, 512], P(None, 'ch'), may hold values from 13556.588 to 54226.35
- actbias: float32 [2, 512], P(None, 'ch'), may hold values from -3 to 3
- actbias_mean: float32 [2, 512], P(None, 'ch'), may hold values from -1028.7736 to 1028.7736
- actbias_square: float32 [2, 512], P(None, 'ch'), may hold values from 54224.426 to 216897.7
- rgbmix: float32 [3, 512], P(None, 'ch'), may hold values from -6 to 6
- rgbmix_mean: float32 [3, 512], P(None, 'ch'), may hold values from -363.73035 to 363.73035
- rgbmix_square: float32 [3, 512], P(None, 'ch'), may hold values from 6778.202 to 27112.809
- scalars: float32 [5], replicated, may hold values from -3 to 3
- scalars_mean: float32 [5], replicated, may hold values from -13967.032 to 13967.032
- scalars_square: float32 [5], replicated, may hold values from 238.2889 to 39978243, as said below
Outputs:
- features_grad: float32 [512, 64, 1024], P('ch', 'img')
- upsampler_stepped: float32 [512, 9, 512], P('ch', None, 'img')
- upsampler_moment: float32 [512, 9, 512], P('ch', None, 'img')
- upsampler_variance: float32 [512, 9, 512], P('ch', None, 'img')
- refiner_stepped: float32 [512, 9, 512], P('ch', None, 'img')
- refiner_moment: float32 [512, 9, 512], P('ch', None, 'img')
- refiner_variance: float32 [512, 9, 512], P('ch', None, 'img')
- affines_stepped: float32 [3, 512, 512], P(None, 'img', 'ch')
- affines_moment: float32 [3, 512, 512], P(None, 'img', 'ch')
- affines_variance: float32 [3, 512, 512], P(None, 'img', 'ch')
- modbias_stepped: float32 [3, 512], P(None, 'ch')
- modbias_moment: float32 [3, 512], P(None, 'ch')
- modbias_variance: float32 [3, 512], P(None, 'ch')
- actbias_stepped: float32 [2, 512], P(None, 'ch')
- actbias_moment: float32 [2, 512], P(None, 'ch')
- actbias_variance: float32 [2, 512], P(None, 'ch')
- rgbmix_stepped: float32 [3, 512], P(None, 'ch')
- rgbmix_moment: float32 [3, 512], P(None, 'ch')
- rgbmix_variance: float32 [3, 512], P(None, 'ch')
- scalars_stepped: float32 [5], replicated
- scalars_moment: float32 [5], replicated
- scalars_variance: float32 [5], replicated
The draws below stay inside these ranges and needn't reach their ends.
Inputs may be any that keep to these rules, and one draw needn't show every extreme that they name: `scalars_square`: positive.
All inputs are finite; a program needn't handle non-finite values. No bound on the sum of `crop_mask` on one device may be relied on, other than what follows from the above.
Results may differ from the reference program's by a relative error of at most 0.006.
The reference program's roundings to bfloat16 on the way count: a program that leaves them out, or rounds other values in their place, can miss the bound.
Values may be sent and summed in bfloat16 or wider, within the bound.
No kernel may reach another device: no remote copies, remote signals or barrier semaphores. Data moves between devices by JAX's collectives and lax.ppermute only.
A program may use at most 576 MiB of HBM per device.

```python
import math
import jax
import jax.numpy as jnp
from jax import lax

C = 512
WDIM = 512
RES = 32
CRITIC = 64
STEP = 10
IMAGES = 64
PIXELS = 4096


def scalar_scales():
    noise_scale = 0.3 * (PIXELS * IMAGES) ** 0.5
    color_scale = 0.12 * PIXELS * IMAGES
    return jnp.array([noise_scale, noise_scale, color_scale, color_scale, color_scale], jnp.float32)


def draw_scalars_mean(key, part):
    normal_draw = jnp.clip(jax.random.normal(jax.random.fold_in(key, 11), (5,), jnp.float32), -4.0, 4.0)
    return normal_draw * 0.111 * scalar_scales()


def draw_scalars_square(key, part):
    spread = jax.random.uniform(jax.random.fold_in(key, 12), (5,), jnp.float32, math.log(0.0101), math.log(0.0404))
    return jnp.exp(spread) * scalar_scales() * scalar_scales()


def with_ends(result, key, low, high):
    longest = result.shape.index(max(result.shape))
    spots = []
    for shift in (0, 1):
        where = [jax.random.randint(jax.random.fold_in(key, axis), (), 0, length) for axis, length in enumerate(result.shape)]
        where[longest] = (where[longest] + shift) % result.shape[longest]
        spots.append(tuple(where))
    return result.at[spots[0]].set(low).at[spots[1]].set(high)


def shard_levels(rng, shape, cuts, low, high):
    level, own = 1.0, jax.random.fold_in(rng, 6)
    for dim, blocks in cuts:
        draws = jnp.exp(jax.random.uniform(jax.random.fold_in(own, dim), (blocks,), jnp.float32, low / len(cuts), high / len(cuts)))
        level = level * jnp.repeat(draws, shape[dim] // blocks).reshape([-1 if axis == dim else 1 for axis in range(len(shape))])
    return level


def noise(rng, extent, width, limit, split=(), kind=jnp.bfloat16):
    result = width * jax.random.normal(rng, extent, jnp.float32)
    if split:
        result = result * shard_levels(rng, extent, split, -0.22, 0.18)
    return jnp.clip(result, -limit, limit).astype(kind)


def setup_inputs(seed: int = 0) -> dict:
    key_of = jax.random.split(jax.random.key(seed), 31)
    return {
        "features": noise(key_of[0], (C, IMAGES, RES * RES), 1.0, 6.0, ((0, 2), (1, 16))),
        "latents": noise(key_of[1], (IMAGES, WDIM), 1.0, 6.0, ((0, 16),)),
        "skip_rgb": noise(key_of[2], (3, IMAGES, RES * RES), 1.0, 6.0, ((1, 16),), jnp.float32),
        "noises": noise(key_of[3], (2, IMAGES, PIXELS), 1.0, 6.0, ((1, 16),), jnp.float32),
        "ada_shift": with_ends(jax.random.randint(key_of[4], (IMAGES, 2), 0 - RES // 4, RES // 4 + 1), jax.random.fold_in(key_of[4], 1), 0 - RES // 4, (RES // 4 + 1) - 1).astype(jnp.int32),
        "crop_mask": with_ends((jax.random.randint(key_of[5], (IMAGES, PIXELS), 0, 4) < 3).astype(jnp.int32), jax.random.fold_in(key_of[5], 1), 0, 1),
        "critic_mix": noise(key_of[6], (CRITIC, 3), 3 ** -0.5, 3.5, (), jnp.float32),
        "critic_bias": noise(key_of[7], (CRITIC,), 0.5, 3.0, (), jnp.float32),
        "critic_out": noise(key_of[8], (CRITIC,), CRITIC ** -0.5, 0.75, (), jnp.float32),
        "upsampler": noise(key_of[9], (C, 9, C), 1.0, 6.0, ((0, 2), (2, 16)), jnp.float32),
        "upsampler_mean": noise(key_of[10], (C, 9, C), (0.111 * 0.05 * (PIXELS * IMAGES) ** 0.5 / C), 0.0222, ((0, 2), (2, 16)), jnp.float32),
        "upsampler_square": jnp.clip(jnp.exp(math.log(0.000101) - 1.3862944 * jax.random.uniform(key_of[11], (C, 9, C), jnp.float32) ** shard_levels(key_of[11], (C, 9, C), ((0, 2), (2, 16)), -0.2, 0.2)), 2.5249999453080818e-05, 0.000101),
        "refiner": noise(key_of[12], (C, 9, C), 1.0, 6.0, ((0, 2), (2, 16)), jnp.float32),
        "refiner_mean": noise(key_of[13], (C, 9, C), (0.111 * (0.0196 * PIXELS * IMAGES + 0.0005 * PIXELS * IMAGES * PIXELS * IMAGES) ** 0.5 / C), 5.0835886, ((0, 2), (2, 16)), jnp.float32),
        "refiner_square": jnp.clip(jnp.exp(math.log(5.2961006) - 1.3862944 * jax.random.uniform(key_of[14], (C, 9, C), jnp.float32) ** shard_levels(key_of[14], (C, 9, C), ((0, 2), (2, 16)), -0.2, 0.2)), 1.3240252, 5.2961006),
        "affines": noise(key_of[15], (3, WDIM, C), 1.0, 6.0, ((1, 16), (2, 2)), jnp.float32),
        "affines_mean": noise(key_of[16], (3, WDIM, C), (0.111 * ((0.1156 * PIXELS * IMAGES + 0.01 * PIXELS * PIXELS * IMAGES) / (C * WDIM)) ** 0.5), 2.845607, ((1, 16), (2, 2)), jnp.float32),
        "affines_square": jnp.clip(jnp.exp(math.log(1.6594542) - 1.3862944 * jax.random.uniform(key_of[17], (3, WDIM, C), jnp.float32) ** shard_levels(key_of[17], (3, WDIM, C), ((1, 16), (2, 2)), -0.2, 0.2)), 0.41486356, 1.6594542),
        "modbias": jnp.clip(1.0 + 0.1 * jax.random.normal(key_of[18], (3, C), jnp.float32), 0.5, 1.5),
        "modbias_mean": noise(key_of[19], (3, C), (0.111 * ((0.1156 * PIXELS * IMAGES + 0.01 * PIXELS * IMAGES * PIXELS * IMAGES) / C) ** 0.5), 514.3959, ((1, 2),), jnp.float32),
        "modbias_square": jnp.clip(jnp.exp(math.log(54226.35) - 1.3862944 * jax.random.uniform(key_of[20], (3, C), jnp.float32) ** shard_levels(key_of[20], (3, C), ((1, 2),), -0.2, 0.2)), 13556.588, 54226.35),
        "actbias": noise(key_of[21], (2, C), 0.5, 3.0, ((1, 2),), jnp.float32),
        "actbias_mean": noise(key_of[22], (2, C), (0.111 * ((0.09 * PIXELS * IMAGES + 0.04 * PIXELS * IMAGES * PIXELS * IMAGES) / C) ** 0.5), 1028.7736, ((1, 2),), jnp.float32),
        "actbias_square": jnp.clip(jnp.exp(math.log(216897.7) - 1.3862944 * jax.random.uniform(key_of[23], (2, C), jnp.float32) ** shard_levels(key_of[23], (2, C), ((1, 2),), -0.2, 0.2)), 54224.426, 216897.7),
        "rgbmix": noise(key_of[24], (3, C), 1.0, 6.0, ((1, 2),), jnp.float32),
        "rgbmix_mean": noise(key_of[25], (3, C), (0.111 * ((0.04 * PIXELS * IMAGES + 0.005 * PIXELS * IMAGES * PIXELS * IMAGES) / C) ** 0.5), 363.73035, ((1, 2),), jnp.float32),
        "rgbmix_square": jnp.clip(jnp.exp(math.log(27112.809) - 1.3862944 * jax.random.uniform(key_of[26], (3, C), jnp.float32) ** shard_levels(key_of[26], (3, C), ((1, 2),), -0.2, 0.2)), 6778.202, 27112.809),
        "scalars": noise(key_of[27], (5,), 0.5, 3.0, (), jnp.float32),
        "scalars_mean": draw_scalars_mean(jax.random.fold_in(key_of[30], 71), 0),
        "scalars_square": draw_scalars_square(jax.random.fold_in(key_of[30], 71), 0),
    }


PRECISE = lax.Precision.HIGHEST
ROOT_TWO = 1.4142135623730951
BETA_ONE = 0.9
BETA_TWO = 0.99
LEARN_RATE = 0.3
DECAY_RATE = 0.01
ADAM_EPS = 1e-08
DEMOD_EPS = 1e-08
TAP_OFFSETS = ((-1, -1), (-1, 0), (-1, 1), (0, -1), (0, 0), (0, 1), (1, -1), (1, 0), (1, 1))

@jax.custom_vjp
def low(v):
    return lax.optimization_barrier(v.astype(jnp.bfloat16)).astype(jnp.float32)

@jax.custom_vjp
def low_back(v):
    return v

def low_keep(v):
    return (low(v), None)

def low_pass(kept, grad):
    return (grad,)

def back_keep(v):
    return (v, None)

def back_low(kept, grad):
    return (low(grad),)
low.defvjp(low_keep, low_pass)
low_back.defvjp(back_keep, back_low)

def shift_grid(values, off_row, off_col, grid_side):
    total_pixels = grid_side * grid_side
    moved_by = off_row * grid_side + off_col
    leading = values.shape[:-1]
    if moved_by > 0:
        shifted = jnp.concatenate([values[..., moved_by:], jnp.zeros(leading + (moved_by,), values.dtype)], axis=-1)
    elif moved_by < 0:
        shifted = jnp.concatenate([jnp.zeros(leading + (-moved_by,), values.dtype), values[..., :moved_by]], axis=-1)
    else:
        shifted = values
    if off_col != 0:
        column = jnp.arange(total_pixels, dtype=jnp.int32) % grid_side
        inside = (column + off_col >= 0) & (column + off_col < grid_side)
        shifted = jnp.where(inside, shifted, jnp.zeros((), values.dtype))
    return shifted

def leaky(values):
    return 0.2 * values + 0.8 * jax.nn.softplus(values)

def conv_same(inputs, kernel, grid_side):
    summed = jnp.zeros((kernel.shape[2],) + inputs.shape[1:], jnp.float32)
    for number, offsets in enumerate(TAP_OFFSETS):
        summed = summed + jnp.einsum('io,ibp->obp', kernel[:, number, :], shift_grid(inputs, offsets[0], offsets[1], grid_side), precision=PRECISE)
    return summed

def zero_insert(inputs, grid_side):
    channels, images = (inputs.shape[0], inputs.shape[1])
    lattice = inputs.reshape(channels, images, grid_side, 1, grid_side, 1)
    spread = jnp.concatenate([lattice, jnp.zeros_like(lattice)], axis=5)
    spread = jnp.concatenate([spread, jnp.zeros_like(spread)], axis=3)
    return spread.reshape(channels, images, 4 * grid_side * grid_side)

def upsample_skip(planes, grid_side):
    lattice = planes.reshape(planes.shape[0], planes.shape[1], grid_side, 1, grid_side, 1)
    lattice = jnp.broadcast_to(lattice, (planes.shape[0], planes.shape[1], grid_side, 2, grid_side, 2))
    return lattice.reshape(planes.shape[0], planes.shape[1], 4 * grid_side * grid_side)

def translate(planes, shift_pairs, direction, grid_side):

    def single(plane, shift_pair):
        lattice = plane.reshape(plane.shape[0], grid_side, grid_side)
        lattice = jnp.roll(lattice, direction * shift_pair[0], axis=1)
        lattice = jnp.roll(lattice, direction * shift_pair[1], axis=2)
        return lattice.reshape(plane.shape[0], grid_side * grid_side)
    return jax.vmap(single, in_axes=(1, 0), out_axes=1)(planes, shift_pairs)

def block_loss(params, features_in, latent, skip_plane, noise_plane, shift_pair, mask_plane, critic):
    upsampler, refiner, affines, modbias, actbias, rgbmix, scalars = params
    critic_mix, critic_bias, critic_out = critic
    up_low = low(upsampler)
    ref_low = low(refiner)
    aff_low = low(affines)
    style_gain = affines.shape[1] ** (-0.5)

    def style(number):
        return low_back(jnp.dot(latent, aff_low[number], precision=PRECISE) * style_gain + modbias[number][None, :])

    def demod(styles, kernel):
        weight_sq = lax.optimization_barrier(jnp.sum(kernel * kernel, axis=1))
        return lax.rsqrt(jnp.dot(styles * styles, weight_sq, precision=PRECISE) + DEMOD_EPS)
    style_one = style(0)
    mod_one = low(features_in * style_one.T[:, :, None])
    raw_one = low_back(conv_same(zero_insert(mod_one, RES), up_low, 2 * RES))
    pre_one = raw_one * demod(style_one, up_low).T[:, :, None] + scalars[0] * noise_plane[0][None] + actbias[0][:, None, None]
    act_one = leaky(pre_one) * ROOT_TWO
    style_two = style(1)
    mod_two = low(act_one * style_two.T[:, :, None])
    raw_two = low_back(conv_same(mod_two, ref_low, 2 * RES))
    pre_two = raw_two * demod(style_two, ref_low).T[:, :, None] + scalars[1] * noise_plane[1][None] + actbias[1][:, None, None]
    act_two = leaky(pre_two) * ROOT_TWO
    style_three = style(2)
    mod_three = low(act_two * style_three.T[:, :, None])
    rgb_low = low(rgbmix * rgbmix.shape[1] ** (-0.5))
    colors = low_back(jnp.einsum('ci,ibp->cbp', rgb_low, mod_three, precision=PRECISE))
    colors = colors + scalars[2:5][:, None, None] + upsample_skip(skip_plane, RES)
    moved = translate(colors, shift_pair, 1, 2 * RES)
    hidden = jnp.einsum('kc,cbp->kbp', critic_mix, moved, precision=PRECISE) + critic_bias[:, None, None]
    logits = jnp.einsum('k,kbp->bp', critic_out, leaky(hidden), precision=PRECISE)
    return jnp.sum(mask_plane * jax.nn.softplus(-logits))

def adam_step(weight, mean_old, square_old, gradient, count):
    moment = BETA_ONE * mean_old + (1.0 - BETA_ONE) * gradient
    variance = BETA_TWO * square_old + (1.0 - BETA_TWO) * gradient * gradient
    fix_one = 1.0 - BETA_ONE ** count
    fix_two = 1.0 - BETA_TWO ** count
    update = moment / fix_one / (jnp.sqrt(variance / fix_two) + ADAM_EPS) + DECAY_RATE * weight
    return (weight - LEARN_RATE * update, moment, variance)

def reference(features, latents, skip_rgb, noises, ada_shift, crop_mask, critic_mix, critic_bias, critic_out, upsampler, upsampler_mean, upsampler_square, refiner, refiner_mean, refiner_square, affines, affines_mean, affines_square, modbias, modbias_mean, modbias_square, actbias, actbias_mean, actbias_square, rgbmix, rgbmix_mean, rgbmix_square, scalars, scalars_mean, scalars_square):
    params = (upsampler, refiner, affines, modbias, actbias, rgbmix, scalars)
    critic = (critic_mix, critic_bias, critic_out)
    records = (jnp.moveaxis(features, 1, 0), latents, jnp.moveaxis(skip_rgb, 1, 0), jnp.moveaxis(noises, 1, 0), ada_shift, crop_mask)

    def one_image(totals, record):
        feature, latent, skip_plane, noise_plane, shift_pair, mask_plane = record

        def image_loss(weights, inputs):
            return block_loss(weights, inputs, latent[None].astype(jnp.float32), skip_plane[:, None, :], noise_plane[:, None, :], shift_pair[None], mask_plane[None].astype(jnp.float32), critic)
        loss_value, pullback = jax.vjp(image_loss, params, feature[:, None, :].astype(jnp.float32))
        gradients, feature_grad = pullback(jnp.ones_like(loss_value))
        return (jax.tree.map(jnp.add, totals, gradients), feature_grad[:, 0, :])
    totals, feature_grads = lax.scan(one_image, jax.tree.map(jnp.zeros_like, params), records)
    count = float(STEP)
    up_new = adam_step(upsampler, upsampler_mean, upsampler_square, totals[0], count)
    ref_new = adam_step(refiner, refiner_mean, refiner_square, totals[1], count)
    aff_new = adam_step(affines, affines_mean, affines_square, totals[2], count)
    mod_new = adam_step(modbias, modbias_mean, modbias_square, totals[3], count)
    act_new = adam_step(actbias, actbias_mean, actbias_square, totals[4], count)
    rgb_new = adam_step(rgbmix, rgbmix_mean, rgbmix_square, totals[5], count)
    scal_new = adam_step(scalars, scalars_mean, scalars_square, totals[6], count)
    return (jnp.moveaxis(feature_grads, 0, 1), up_new[0], up_new[1], up_new[2], ref_new[0], ref_new[1], ref_new[2], aff_new[0], aff_new[1], aff_new[2], mod_new[0], mod_new[1], mod_new[2], act_new[0], act_new[1], act_new[2], rgb_new[0], rgb_new[1], rgb_new[2], scal_new[0], scal_new[1], scal_new[2])
```

```python
import functools

import jax
import jax.numpy as jnp
from jax import lax
from jax.experimental import pallas as pl
from jax.experimental.pallas import tpu as pltpu
from jax.sharding import PartitionSpec as P

C = 512
RES = 32
STEP = 10

PRECISE = lax.Precision.HIGHEST
ROOT_TWO = 1.4142135623730951
BETA_ONE = 0.9
BETA_TWO = 0.99
LEARN_RATE = 0.3
DECAY_RATE = 0.01
ADAM_EPS = 1e-08
DEMOD_EPS = 1e-08
VMEM_LIMIT = 60 * 2**20
BOTH = ("img", "ch")

PAD = RES
PIX = RES * RES
ROWS = PIX + 2 * PAD
TILE = 256
TAPS = tuple((3 * (dy + 1) + dx + 1, dy, dx) for dy in (-1, 0, 1) for dx in (-1, 0, 1))
UP_TAPS = (
    ((4, 0, 0),),
    ((3, 0, 0), (5, 1, 0)),
    ((1, 0, 0), (7, 0, 1)),
    ((0, 0, 0), (2, 1, 0), (6, 0, 1), (8, 1, 1)),
)
NT = (((1,), (1,)), ((), ()))
TN = (((0,), (0,)), ((), ()))
NN = (((1,), (0,)), ((), ()))


def params(**more):
    return pltpu.CompilerParams(vmem_limit_bytes=VMEM_LIMIT, **more)


def mul(left, right, dims):
    return lax.dot_general(left, right, dims, preferred_element_type=jnp.float32)


def exact(left, right, dims):
    return lax.dot_general(
        left, right, dims, precision=PRECISE, preferred_element_type=jnp.float32
    )


def softplus(values):
    return jnp.maximum(values, 0.0) + jnp.log(1.0 + jnp.exp(-jnp.abs(values)))


def activate(values):
    return (0.2 * ROOT_TWO) * values + (0.8 * ROOT_TWO) * softplus(values)


def slope(values):
    return 0.6 + 0.4 * jnp.tanh(0.5 * values)


def side_copy(values, odd):
    column = lax.broadcasted_iota(jnp.int32, values.shape, 0) & (RES - 1)
    if odd:
        return jnp.where(column == 0, 0.0, pltpu.roll(values, 1, 0))
    return jnp.where(column == RES - 1, 0.0, pltpu.roll(values, values.shape[0] - 1, 0))


def column_sums(values):
    return jnp.sum(values, axis=0, keepdims=True)


def square_sums(weight_ref, out_ref):
    chans = weight_ref.shape[1]
    for start in range(0, chans, 64):
        total = None
        for tap in range(9):
            part = weight_ref[tap, pl.ds(start, 64), :].astype(jnp.float32)
            total = part * part if total is None else total + part * part
        out_ref[pl.ds(start, 64), :] = total


def demod_of(style, squares):
    spread = jnp.broadcast_to(style * style, (8, style.shape[1]))
    return lax.rsqrt(exact(spread, squares, NT)[0:1] + DEMOD_EPS)


def phase_taps(row_parity, col_parity, sign):
    found = []
    for tap, dy, dx in TAPS:
        across = col_parity + sign * dx + 2
        down = row_parity + sign * dy + 2
        copy = 1 if across in (1, 4) else 0
        phase = 2 * (down & 1) + (across & 1)
        first = PAD * (down >> 1)
        found.append((tap, phase, copy, first))
    return found


def tap_rows(ref, phase, copy, first, offset, count):
    start = first + offset
    if not isinstance(start, int):
        start = pl.multiple_of(start, PAD)
    return ref[0, phase, copy, pl.ds(start, count), :]


def write_map(ref, phase, rows_at, values, odd):
    ref[0, phase, 0, rows_at, :] = values.astype(jnp.bfloat16)
    ref[0, phase, 1, rows_at, :] = side_copy(values, odd).astype(jnp.bfloat16)


def clear_pads(ref, phase, both=True):
    empty = jnp.zeros((PAD, ref.shape[-1]), jnp.bfloat16)
    for copy in (0, 1):
        ref[0, phase, copy, 0:PAD, :] = empty
        if both:
            ref[0, phase, copy, PAD + PIX :, :] = empty


def up_forward(
    scal_ref, feat_ref, vec_ref, noise_ref, weight_ref, raw_ref, map_ref, xs_ref, sq_ref, demod_ref
):
    @pl.when(pl.program_id(0) == 0)
    def _():
        square_sums(weight_ref, sq_ref)

    style_one = vec_ref[0, 0:1, :]
    style_two = vec_ref[0, 1:2, :]
    bias = vec_ref[0, 3:4, :]
    demod = demod_of(style_one, sq_ref[...])
    demod_ref[0] = jnp.broadcast_to(demod, demod_ref.shape[1:])
    chans = feat_ref.shape[-1]
    for start in range(0, PIX, TILE):
        values = feat_ref[0, pl.ds(start, TILE), :].astype(jnp.float32) * style_one
        xs_ref[0, 0, pl.ds(start, TILE), :] = values.astype(jnp.bfloat16)
        xs_ref[0, 1, pl.ds(start, TILE), :] = side_copy(values, False).astype(jnp.bfloat16)
    xs_ref[0, 0, PIX:, :] = jnp.zeros((PAD, chans), jnp.bfloat16)
    xs_ref[0, 1, PIX:, :] = jnp.zeros((PAD, chans), jnp.bfloat16)
    strength = scal_ref[0]
    for phase in range(4):
        noise_cols = jnp.transpose(noise_ref[0, 0, phase // 2]) * strength
        clear_pads(map_ref, phase)
        for start in range(0, PIX, TILE):
            raw = None
            for tap, col_step, row_step in UP_TAPS[phase]:
                part = mul(
                    xs_ref[0, col_step, pl.ds(start + PAD * row_step, TILE), :], weight_ref[tap], NT
                )
                raw = part if raw is None else raw + part
            raw_ref[0, phase, pl.ds(start, TILE), :] = raw
            noise = noise_cols[start : start + TILE, phase % 2 : phase % 2 + 1]
            pre = raw * demod + noise + bias
            write_map(
                map_ref, phase, pl.ds(PAD + start, TILE), activate(pre) * style_two, phase % 2 == 1
            )


def flat_forward(
    scal_ref,
    map_ref,
    vec_ref,
    noise_ref,
    base_ref,
    mask_ref,
    critic_ref,
    rgb_ref,
    weight_ref,
    grad_ref,
    sums_ref,
    color_ref,
    raw_buf,
    slope_buf,
    act_buf,
    sq_buf,
):
    row_parity = pl.program_id(1)

    @pl.when((pl.program_id(0) == 0) & (row_parity == 0))
    def _():
        square_sums(weight_ref, sq_buf)

    @pl.when(row_parity == 0)
    def _():
        sums_ref[...] = jnp.zeros_like(sums_ref)
        color_ref[...] = jnp.zeros_like(color_ref)

    style_two = vec_ref[0, 1:2, :]
    style_three = vec_ref[0, 2:3, :]
    bias = vec_ref[0, 4:5, :]
    demod = demod_of(style_two, sq_buf[...])
    strength = scal_ref[1]
    noise_all = jnp.transpose(noise_ref[0, 0, 0])
    rgb = rgb_ref[...]
    for col_parity in (0, 1):
        taps = phase_taps(row_parity, col_parity, 1)
        lines = []
        for start in range(0, PIX, TILE):
            raw = None
            for tap, phase, copy, first in taps:
                part = mul(
                    tap_rows(map_ref, phase, copy, first, start, TILE), weight_ref[tap], NT
                )
                raw = part if raw is None else raw + part
            here = pl.ds(start, TILE)
            raw_buf[here, :] = raw
            noise = noise_all[start : start + TILE, col_parity : col_parity + 1]
            pre = raw * demod + strength * noise + bias
            act = activate(pre)
            act_buf[here, :] = act
            slope_buf[here, :] = slope(pre)
            lines.append(mul(rgb, (act * style_three).astype(jnp.bfloat16), NT))
        colors = jnp.concatenate(lines, axis=1)[0:8] + base_ref[0]
        mix = critic_ref[...]
        hidden = mix[:, 3:4]
        for color in range(3):
            hidden = hidden + mix[:, color : color + 1] * colors[color : color + 1]
        out = mix[:, 4:5]
        unit = 0.2 * hidden + 0.8 * softplus(hidden)
        logits = column_sums(out * unit)
        mask = mask_ref[0, 0, col_parity : col_parity + 1, :]
        grad_logits = -mask / (1.0 + jnp.exp(logits))
        grad_hidden = out * grad_logits * slope(hidden)
        grad_colors = jnp.concatenate(
            [column_sums(mix[:, color : color + 1] * grad_hidden) for color in range(3)]
            + [jnp.zeros((5, PIX), jnp.float32)],
            axis=0,
        )
        total = None
        for lane in range(0, PIX, 128):
            piece = grad_colors[:, lane : lane + 128]
            total = piece if total is None else total + piece
        color_ref[0] += total
        grad_low = jnp.concatenate(
            [grad_colors, jnp.zeros((8, PIX), jnp.float32)], axis=0
        ).astype(jnp.bfloat16)
        clear_pads(grad_ref, col_parity)
        sums = [None] * 4
        rgb_sum = None
        for start in range(0, PIX, TILE):
            here = pl.ds(start, TILE)
            colors_here = grad_low[:, start : start + TILE]
            grad_map = mul(colors_here, rgb, TN)
            act = act_buf[here, :]
            grad_pre = grad_map * (style_three * ROOT_TWO) * slope_buf[here, :]
            write_map(grad_ref, col_parity, pl.ds(PAD + start, TILE), grad_pre * demod, col_parity == 1)
            noise = noise_all[start : start + TILE, col_parity : col_parity + 1]
            found = (
                column_sums(grad_map * act),
                column_sums(grad_pre * raw_buf[here, :]),
                column_sums(grad_pre),
                column_sums(grad_pre * noise),
            )
            sums = [f if s is None else s + f for s, f in zip(sums, found)]
            mixed = mul(colors_here, (act * style_three).astype(jnp.bfloat16), NN)
            rgb_sum = mixed if rgb_sum is None else rgb_sum + mixed
        for row in range(4):
            sums_ref[0, row : row + 1, :] += sums[row]
        sums_ref[0, 8:16, :] += rgb_sum[0:8]

    @pl.when(row_parity == 1)
    def _():
        coef = -0.5 * demod * demod * demod * sums_ref[0, 1:2, :]
        sums_ref[0, 4:5, :] = coef
        back = exact(jnp.broadcast_to(coef, (8, coef.shape[1])), sq_buf[...], NN)[0:1]
        sums_ref[0, 5:6, :] = 2.0 * style_two * back


def spread_out(acc_ref, weight_ref, coef_ref, style_ref, out_ref):
    squares = exact(coef_ref[...], style_ref[...], TN)
    blocks, _, rows, cols = out_ref.shape
    if len(out_ref.shape) == 4 and cols % 128 == 0:
        across = weight_ref.shape[2] // cols
        for tap in range(9):
            grad = acc_ref[tap] + 2.0 * weight_ref[tap].astype(jnp.float32) * squares
            for block in range(blocks):
                row, col = (block // across) * rows, (block % across) * cols
                out_ref[block, tap] = grad[row : row + rows, col : col + cols].astype(out_ref.dtype)
    else:
        for tap in range(9):
            grad = acc_ref[tap] + 2.0 * weight_ref[tap].astype(jnp.float32) * squares
            out_ref[0, tap] = grad.astype(out_ref.dtype)


def flat_weight(grad_ref, map_ref, weight_ref, coef_ref, style_ref, out_ref, acc_ref):
    row_parity = pl.program_id(1)

    @pl.when((pl.program_id(0) == 0) & (row_parity == 0))
    def _():
        acc_ref[...] = jnp.zeros_like(acc_ref)

    for col_parity in (0, 1):
        grad = grad_ref[0, col_parity, 0, PAD : PAD + PIX, :]
        for tap, phase, copy, first in phase_taps(row_parity, col_parity, 1):
            acc_ref[tap] += mul(grad, tap_rows(map_ref, phase, copy, first, 0, PIX), TN)

    @pl.when((pl.program_id(0) == pl.num_programs(0) - 1) & (row_parity == 1))
    def _():
        spread_out(acc_ref, weight_ref, coef_ref, style_ref, out_ref)


def up_weight(grad_ref, xs_ref, weight_ref, coef_ref, style_ref, out_ref, acc_ref):
    @pl.when(pl.program_id(0) == 0)
    def _():
        acc_ref[...] = jnp.zeros_like(acc_ref)

    for phase in range(4):
        grad = grad_ref[0, phase, 0, PAD:, :]
        for tap, col_step, row_step in UP_TAPS[phase]:
            acc_ref[tap] += mul(grad, xs_ref[0, col_step, pl.ds(PAD * row_step, PIX), :], TN)

    @pl.when(pl.program_id(0) == pl.num_programs(0) - 1)
    def _():
        spread_out(acc_ref, weight_ref, coef_ref, style_ref, out_ref)


def flat_back(
    scal_ref, grad_ref, raw_ref, vec_ref, demod_ref, noise_ref, weight_ref, out_ref, sums_ref
):
    row_parity = pl.program_id(1)

    @pl.when(row_parity == 0)
    def _():
        sums_ref[...] = jnp.zeros_like(sums_ref)

    style_two = vec_ref[0, 1:2, :]
    bias = vec_ref[0, 3:4, :]
    demod = demod_ref[0, 0:1, :]
    strength = scal_ref[0]
    noise_all = jnp.transpose(noise_ref[0, 0, 0])
    for col_parity in (0, 1):
        taps = phase_taps(row_parity, col_parity, -1)
        clear_pads(out_ref, col_parity, False)
        sums = [None] * 4
        for start in range(0, PIX, TILE):
            grad_map = None
            for tap, phase, copy, first in taps:
                part = mul(
                    tap_rows(grad_ref, phase, copy, first, start, TILE), weight_ref[tap], NN
                )
                grad_map = part if grad_map is None else grad_map + part
            raw = raw_ref[0, col_parity, pl.ds(start, TILE), :]
            noise = noise_all[start : start + TILE, col_parity : col_parity + 1]
            pre = raw * demod + strength * noise + bias
            grad_pre = grad_map * (style_two * ROOT_TWO) * slope(pre)
            write_map(out_ref, col_parity, pl.ds(PAD + start, TILE), grad_pre * demod, col_parity == 1)
            found = (
                column_sums(grad_map * activate(pre)),
                column_sums(grad_pre * raw),
                column_sums(grad_pre),
                column_sums(grad_pre * noise),
            )
            sums = [f if s is None else s + f for s, f in zip(sums, found)]
        for row in range(4):
            sums_ref[0, row : row + 1, :] += sums[row]


def up_back(grad_ref, feat_ref, vec_ref, weight_ref, out_ref, sums_ref):
    style_one = vec_ref[0, 0:1, :]
    total = None
    for start in range(0, PIX, TILE):
        grad_map = None
        for phase in range(4):
            for tap, col_step, row_step in UP_TAPS[phase]:
                rows = grad_ref[0, phase, col_step, pl.ds(PAD + start - PAD * row_step, TILE), :]
                part = mul(rows, weight_ref[tap], NN)
                grad_map = part if grad_map is None else grad_map + part
        found = column_sums(grad_map * feat_ref[0, pl.ds(start, TILE), :].astype(jnp.float32))
        total = found if total is None else total + found
        out_ref[0, :, pl.ds(start, TILE)] = jnp.transpose(grad_map * style_one)
    sums_ref[0] = jnp.broadcast_to(total, sums_ref.shape[1:])


def whole(shape):
    zeros = (0,) * len(shape)
    return pl.BlockSpec(shape, lambda *ids: zeros)


def per_image(shape):
    zeros = (0,) * (len(shape) - 1)
    return pl.BlockSpec((1,) + tuple(shape[1:]), lambda image, *ids: (image,) + zeros)


SMEM = pl.BlockSpec(memory_space=pltpu.SMEM)


def cost(flops, moved):
    return pl.CostEstimate(flops=int(flops), bytes_accessed=int(moved), transcendentals=0)


def half_phases(shape):
    zeros = (0,) * (len(shape) - 2)
    return pl.BlockSpec(
        (1, 2) + tuple(shape[2:]), lambda image, parity: (image, parity) + zeros
    )


def noise_spec(layer):
    return pl.BlockSpec((1, 1, 1, 8, PIX), lambda image, parity: (image, layer, parity, 0, 0))


def call_up_forward(scalars, feat, vecs, noise, weight):
    images, _, chans = feat.shape
    out_shape = (
        jax.ShapeDtypeStruct((images, 4, PIX, chans), jnp.float32),
        jax.ShapeDtypeStruct((images, 4, 2, ROWS, chans), jnp.bfloat16),
        jax.ShapeDtypeStruct((images, 2, PIX + PAD, chans), jnp.bfloat16),
        jax.ShapeDtypeStruct((chans, chans), jnp.float32),
        jax.ShapeDtypeStruct((images, 8, chans), jnp.float32),
    )
    return pl.pallas_call(
        up_forward,
        grid=(images,),
        in_specs=[
            SMEM,
            per_image(feat.shape),
            per_image(vecs.shape),
            pl.BlockSpec((1, 1, 2, 8, PIX), lambda image: (image, 0, 0, 0, 0)),
            whole(weight.shape),
        ],
        out_specs=[
            per_image(out_shape[0].shape),
            per_image(out_shape[1].shape),
            per_image(out_shape[2].shape),
            whole(out_shape[3].shape),
            per_image(out_shape[4].shape),
        ],
        out_shape=out_shape,
        compiler_params=params(),
        cost_estimate=cost(18 * images * PIX * chans * chans, 60e6),
        name="up_forward",
    )(scalars, feat, vecs, noise, weight)


def call_flat_forward(scalars, maps, vecs, noise, base, mask, critic, rgb, weight):
    images, chans = maps.shape[0], maps.shape[-1]
    out_shape = (
        jax.ShapeDtypeStruct((images, 4, 2, ROWS, chans), jnp.bfloat16),
        jax.ShapeDtypeStruct((images, 16, chans), jnp.float32),
        jax.ShapeDtypeStruct((images, 8, 128), jnp.float32),
    )
    return pl.pallas_call(
        flat_forward,
        grid=(images, 2),
        in_specs=[
            SMEM,
            per_image(maps.shape),
            per_image(vecs.shape),
            noise_spec(1),
            per_image(base.shape),
            pl.BlockSpec((1, 1, 8, PIX), lambda image, parity: (image, parity, 0, 0)),
            whole(critic.shape),
            whole(rgb.shape),
            whole(weight.shape),
        ],
        out_specs=[
            half_phases(out_shape[0].shape),
            per_image(out_shape[1].shape),
            per_image(out_shape[2].shape),
        ],
        out_shape=out_shape,
        scratch_shapes=[pltpu.VMEM((PIX, chans), jnp.float32)] * 3
        + [pltpu.VMEM((chans, chans), jnp.float32)],
        compiler_params=params(),
        cost_estimate=cost(72 * images * PIX * chans * chans, 60e6),
        name="flat_forward",
    )(scalars, maps, vecs, noise, base, mask, critic, rgb, weight)


def gradient_shape(chans, blocks, rows, cols, dtype):
    if cols % 128 == 0:
        return jax.ShapeDtypeStruct((blocks, 9, rows, cols), dtype)
    return jax.ShapeDtypeStruct((1, 9, chans, chans), dtype)


def call_flat_weight(grad, maps, weight, coef, style_sq, out_shape):
    images, chans = maps.shape[0], maps.shape[-1]
    return pl.pallas_call(
        flat_weight,
        grid=(images, 2),
        in_specs=[
            pl.BlockSpec((1, 2, 1, ROWS, chans), lambda image, parity: (image, parity, 0, 0, 0)),
            per_image(maps.shape),
            whole(weight.shape),
            whole(coef.shape),
            whole(style_sq.shape),
        ],
        out_specs=whole(out_shape.shape),
        out_shape=out_shape,
        scratch_shapes=[pltpu.VMEM((9, chans, chans), jnp.float32)],
        compiler_params=params(),
        cost_estimate=cost(72 * images * PIX * chans * chans, 50e6),
        name="flat_weight",
    )(grad, maps, weight, coef, style_sq)


def call_flat_back(scalars, grad, raw, vecs, demod, noise, weight):
    images, chans = grad.shape[0], grad.shape[-1]
    out_shape = (
        jax.ShapeDtypeStruct((images, 4, 2, PIX + PAD, chans), jnp.bfloat16),
        jax.ShapeDtypeStruct((images, 8, chans), jnp.float32),
    )
    return pl.pallas_call(
        flat_back,
        grid=(images, 2),
        in_specs=[
            SMEM,
            per_image(grad.shape),
            half_phases(raw.shape),
            per_image(vecs.shape),
            per_image(demod.shape),
            noise_spec(0),
            whole(weight.shape),
        ],
        out_specs=[half_phases(out_shape[0].shape), per_image(out_shape[1].shape)],
        out_shape=out_shape,
        compiler_params=params(),
        cost_estimate=cost(72 * images * PIX * chans * chans, 60e6),
        name="flat_back",
    )(scalars, grad, raw, vecs, demod, noise, weight)


def call_up_weight(grad, xs, weight, coef, style_sq, out_shape):
    images, chans = xs.shape[0], xs.shape[-1]
    return pl.pallas_call(
        up_weight,
        grid=(images,),
        in_specs=[
            pl.BlockSpec((1, 4, 1, PIX + PAD, chans), lambda image: (image, 0, 0, 0, 0)),
            per_image(xs.shape),
            whole(weight.shape),
            whole(coef.shape),
            whole(style_sq.shape),
        ],
        out_specs=whole(out_shape.shape),
        out_shape=out_shape,
        scratch_shapes=[pltpu.VMEM((9, chans, chans), jnp.float32)],
        compiler_params=params(),
        cost_estimate=cost(18 * images * PIX * chans * chans, 30e6),
        name="up_weight",
    )(grad, xs, weight, coef, style_sq)


def call_up_back(grad, feat, vecs, weight):
    images, _, chans = feat.shape
    out_shape = (
        jax.ShapeDtypeStruct((images, chans, PIX), jnp.float32),
        jax.ShapeDtypeStruct((images, 8, chans), jnp.float32),
    )
    return pl.pallas_call(
        up_back,
        grid=(images,),
        in_specs=[
            per_image(grad.shape),
            per_image(feat.shape),
            per_image(vecs.shape),
            whole(weight.shape),
        ],
        out_specs=[per_image(out_shape[0].shape), per_image(out_shape[1].shape)],
        out_shape=out_shape,
        compiler_params=params(),
        cost_estimate=cost(18 * images * PIX * chans * chans, 30e6),
        name="up_back",
    )(grad, feat, vecs, weight)


def gather_weight(weight, n_img, n_ch):
    block = jnp.transpose(weight.astype(jnp.bfloat16), (1, 2, 0))
    _, rows, cols = block.shape
    every = lax.all_gather(block, BOTH, axis=0, tiled=False)
    every = every.reshape(n_img, n_ch, 9, rows, cols)
    return jnp.transpose(every, (2, 0, 3, 1, 4)).reshape(9, n_img * rows, n_ch * cols)


def scatter_gradient(grad, n_img, n_ch, rows, cols):
    if grad.shape[0] == 1:
        grad = grad.reshape(9, n_img, rows, n_ch, cols)
        grad = jnp.transpose(grad, (1, 3, 0, 2, 4)).reshape(n_img * n_ch, 9, rows, cols)
    block = lax.psum_scatter(grad, BOTH, scatter_dimension=0, tiled=False)
    return jnp.transpose(block.astype(jnp.float32), (2, 0, 1))


def adam_step(weight, mean_old, square_old, gradient, count):
    moment = BETA_ONE * mean_old + (1.0 - BETA_ONE) * gradient
    variance = BETA_TWO * square_old + (1.0 - BETA_TWO) * gradient * gradient
    fix_one = 1.0 - BETA_ONE**count
    fix_two = 1.0 - BETA_TWO**count
    update = moment / fix_one / (jnp.sqrt(variance / fix_two) + ADAM_EPS) + DECAY_RATE * weight
    return (weight - LEARN_RATE * update, moment, variance)


def phases_of_lanes(side):
    column = jnp.arange(side, dtype=jnp.int32)
    target = (column % 2) * (side // 2) + column // 2
    return (target[:, None] == column[None, :]).astype(jnp.float32)


def padded(values, rows):
    short = rows - values.shape[-2]
    shape = values.shape[:-2] + (short, values.shape[-1])
    return jnp.concatenate([values, jnp.zeros(shape, values.dtype)], axis=-2)


def body(
    n_img,
    n_ch,
    features,
    latents,
    skip_rgb,
    noises,
    ada_shift,
    crop_mask,
    critic_mix,
    critic_bias,
    critic_out,
    upsampler,
    upsampler_mean,
    upsampler_square,
    refiner,
    refiner_mean,
    refiner_square,
    affines,
    affines_mean,
    affines_square,
    modbias,
    modbias_mean,
    modbias_square,
    actbias,
    actbias_mean,
    actbias_square,
    rgbmix,
    rgbmix_mean,
    rgbmix_square,
    scalars,
    scalars_mean,
    scalars_square,
):
    local_chans, group_images = features.shape[0], features.shape[1]
    chans = local_chans * n_ch
    rows_own = upsampler.shape[2]
    side = 2 * RES
    share = max(1, n_ch // group_images)
    images = group_images * share // n_ch
    ch_index = lax.axis_index("ch")
    img_index = lax.axis_index("img")
    first = (ch_index // share) * images
    col_start = ch_index * local_chans

    def mine(values, axis):
        return lax.dynamic_slice_in_dim(values, first, images, axis)

    def my_chans(values, axis):
        return lax.dynamic_slice_in_dim(values, col_start, local_chans, axis)

    up_full = gather_weight(upsampler, n_img, n_ch)
    ref_full = gather_weight(refiner, n_img, n_ch)
    aff_full = lax.all_gather(
        lax.all_gather(affines.astype(jnp.bfloat16), "ch", axis=2, tiled=True), "img", axis=1, tiled=True
    )
    small = lax.all_gather(
        jnp.concatenate([modbias, actbias, rgbmix], axis=0), "ch", axis=1, tiled=True
    )
    lat_all = lax.all_gather(latents, "img", axis=0, tiled=True)
    style_gain = latents.shape[1] ** (-0.5)
    lat_own = mine(latents, 0)
    styles = [
        jnp.dot(lat_own, aff_full[number], preferred_element_type=jnp.float32) * style_gain
        + small[number][None, :]
        for number in range(3)
    ]
    vecs = padded(
        jnp.concatenate(
            [jnp.stack(styles, axis=1), jnp.broadcast_to(small[None, 3:5], (images, 2, chans))], axis=1
        ),
        8,
    )
    rgb_low = padded(small[5:8] * C ** (-0.5), 16).astype(jnp.bfloat16)
    if share == 1:
        feat = lax.all_to_all(features, "ch", split_axis=1, concat_axis=0, tiled=True)
    else:
        feat = mine(lax.all_gather(features, "ch", axis=0, tiled=True), 1)
    feat = jnp.transpose(feat, (1, 2, 0))
    noise = jnp.dot(
        mine(noises, 1).reshape(2 * images * side, side), phases_of_lanes(side), precision=PRECISE
    )
    noise = jnp.transpose(noise.reshape(2, images, RES, 2, 2, RES), (1, 0, 3, 4, 2, 5))
    noise = padded(noise.reshape(images, 2, 2, 2, PIX), 8)
    order = jnp.arange(side, dtype=jnp.int32)
    order = 2 * (order % RES) + order // RES
    shifts = mine(ada_shift, 0)
    picks = [
        (((order[None, :] + shifts[:, axis : axis + 1]) % side)[:, :, None] == jnp.arange(side)).astype(
            jnp.bfloat16
        )
        for axis in (0, 1)
    ]
    mask = mine(crop_mask, 0).reshape(images, side, side).astype(jnp.bfloat16)
    mask = jnp.einsum("byz,bzx->byx", picks[0], mask, preferred_element_type=jnp.bfloat16)
    mask = jnp.einsum("byx,bwx->byw", mask, picks[1], preferred_element_type=jnp.float32) / share
    mask = jnp.transpose(mask.reshape(images, 2, RES, 2, RES), (0, 1, 3, 2, 4))
    mask = padded(mask.reshape(images, 2, 2, PIX), 8)
    base = padded(
        jnp.transpose(mine(skip_rgb, 1), (1, 0, 2)) + scalars[2:5][None, :, None], 8
    )
    critic = jnp.concatenate(
        [critic_mix, critic_bias[:, None], critic_out[:, None], jnp.zeros((critic_mix.shape[0], 3))], axis=1
    )

    raw_one, maps, xs, up_square, demod_one = call_up_forward(scalars, feat, vecs, noise, up_full)
    grad_two, sums_two, color_sums = call_flat_forward(
        scalars, maps, vecs, noise, base, mask, critic, rgb_low, ref_full
    )
    blocks = n_img * n_ch
    out_shape = gradient_shape(chans, blocks, rows_own, local_chans, jnp.float32)
    ref_grad = call_flat_weight(
        grad_two,
        maps,
        ref_full,
        padded(sums_two[:, 4], 8),
        padded(styles[1] * styles[1], 8),
        out_shape,
    )
    ref_grad = scatter_gradient(ref_grad, n_img, n_ch, rows_own, local_chans)
    grad_one, sums_one = call_flat_back(scalars, grad_two, raw_one, vecs, demod_one, noise, ref_full)
    demod_row = demod_one[:, 0]
    coef_one = -0.5 * demod_row * demod_row * demod_row * sums_one[:, 1]
    up_grad = call_up_weight(
        grad_one, xs, up_full, padded(coef_one, 8), padded(styles[0] * styles[0], 8), out_shape
    )
    up_grad = scatter_gradient(up_grad, n_img, n_ch, rows_own, local_chans)
    feat_grad, feat_sums = call_up_back(grad_one, feat, vecs, up_full)
    style_demod_one = 2.0 * styles[0] * jnp.dot(coef_one, up_square, precision=PRECISE)

    if share == 1:
        feat_grad = lax.all_to_all(
            feat_grad.astype(jnp.bfloat16), "ch", split_axis=1, concat_axis=0, tiled=True
        ).astype(jnp.float32)
    else:
        feat_grad = lax.all_gather(feat_grad, "ch", axis=0, tiled=True)[::share] * share
        feat_grad = my_chans(feat_grad, 1)
    features_grad = jnp.transpose(feat_grad, (1, 0, 2))

    style_grads = jnp.stack(
        [feat_sums[:, 0] + style_demod_one, sums_one[:, 0] + sums_two[:, 5], sums_two[:, 0]]
    )
    style_grads = style_grads.astype(jnp.bfloat16).astype(jnp.float32)
    color_sum = jnp.sum(color_sums[:, 0:3], axis=(0, 2))
    scalar_row = jnp.concatenate(
        [
            jnp.sum(sums_one[:, 3])[None],
            jnp.sum(sums_two[:, 3])[None],
            color_sum,
            jnp.zeros((chans - 5,), jnp.float32),
        ]
    )
    packed = jnp.concatenate(
        [
            style_grads.reshape(3 * images, chans),
            jnp.sum(sums_one[:, 2], axis=0)[None],
            jnp.sum(sums_two[:, 2], axis=0)[None],
            jnp.sum(sums_two[:, 8:11], axis=0) * C ** (-0.5),
            scalar_row[None],
        ],
        axis=0,
    )
    every = lax.all_gather(packed, BOTH, axis=0, tiled=False)
    scalar_grad = jnp.sum(every[:, 3 * images + 5, 0:5], axis=0)
    every = my_chans(every, 2)
    small_grad = jnp.sum(every[:, 3 * images : 3 * images + 5], axis=0)
    style_all = every[:, : 3 * images].reshape(n_img, n_ch // share, share, 3, images, local_chans)
    style_all = jnp.transpose(jnp.sum(style_all, axis=2), (2, 0, 1, 3, 4))
    style_all = style_all.reshape(3, n_img * group_images, local_chans)
    lat_rows = affines.shape[1]
    lat_cols = lax.dynamic_slice_in_dim(lat_all, img_index * lat_rows, lat_rows, 1)
    aff_grad = (
        jnp.einsum(
            "bj,kbi->kji", lat_cols, style_all.astype(jnp.bfloat16), preferred_element_type=jnp.float32
        )
        * style_gain
    )
    mod_grad = jnp.sum(style_all, axis=1)

    count = float(STEP)
    up_new = adam_step(upsampler, upsampler_mean, upsampler_square, up_grad, count)
    ref_new = adam_step(refiner, refiner_mean, refiner_square, ref_grad, count)
    aff_new = adam_step(affines, affines_mean, affines_square, aff_grad, count)
    mod_new = adam_step(modbias, modbias_mean, modbias_square, mod_grad, count)
    act_new = adam_step(actbias, actbias_mean, actbias_square, small_grad[0:2], count)
    rgb_new = adam_step(rgbmix, rgbmix_mean, rgbmix_square, small_grad[2:5], count)
    scal_new = adam_step(scalars, scalars_mean, scalars_square, scalar_grad, count)
    return (
        (features_grad,) + up_new + ref_new + aff_new + mod_new + act_new + rgb_new + scal_new
    )


def solution(mesh):
    conv = P("ch", None, "img")
    aff = P(None, "img", "ch")
    row = P(None, "ch")
    images = P(None, "img", None)
    return jax.shard_map(
        functools.partial(body, mesh.shape["img"], mesh.shape["ch"]),
        mesh=mesh,
        in_specs=(P("ch", "img", None), P("img", None), images, images, P("img", None), P("img", None))
        + (P(),) * 3
        + (conv,) * 6
        + (aff,) * 3
        + (row,) * 9
        + (P(),) * 3,
        out_specs=(P("ch", "img", None),) + (conv,) * 6 + (aff,) * 3 + (row,) * 9 + (P(),) * 3,
        check_vma=False,
    )
```

```python
import functools

import jax
import jax.numpy as jnp
from jax import lax
from jax.experimental import pallas as pl
from jax.experimental.pallas import tpu as pltpu
from jax.sharding import PartitionSpec as P

C = 512
RES = 32
STEP = 10

PRECISE = lax.Precision.HIGHEST
ROOT_TWO = 1.4142135623730951
BETA_ONE = 0.9
BETA_TWO = 0.99
LEARN_RATE = 0.3
DECAY_RATE = 0.01
ADAM_EPS = 1e-08
DEMOD_EPS = 1e-08
VMEM_LIMIT = 60 * 2**20
BOTH = ("img", "ch")

PAD = RES
PIX = RES * RES
ROWS = PIX + 2 * PAD
TILE = 256
TAPS = tuple((3 * (dy + 1) + dx + 1, dy, dx) for dy in (-1, 0, 1) for dx in (-1, 0, 1))
UP_TAPS = (
    ((4, 0, 0),),
    ((3, 0, 0), (5, 1, 0)),
    ((1, 0, 0), (7, 0, 1)),
    ((0, 0, 0), (2, 1, 0), (6, 0, 1), (8, 1, 1)),
)
NT = (((1,), (1,)), ((), ()))
TN = (((0,), (0,)), ((), ()))
NN = (((1,), (0,)), ((), ()))


def params(**more):
    return pltpu.CompilerParams(vmem_limit_bytes=VMEM_LIMIT, **more)


def mul(left, right, dims):
    return lax.dot_general(left, right, dims, preferred_element_type=jnp.float32)


def exact(left, right, dims):
    return lax.dot_general(
        left, right, dims, precision=PRECISE, preferred_element_type=jnp.float32
    )


def softplus(values):
    return jnp.maximum(values, 0.0) + jnp.log(1.0 + jnp.exp(-jnp.abs(values)))


def activate(values):
    return (0.2 * ROOT_TWO) * values + (0.8 * ROOT_TWO) * softplus(values)


def slope(values):
    return 0.6 + 0.4 * jnp.tanh(0.5 * values)


def side_copy(values, odd):
    column = lax.broadcasted_iota(jnp.int32, values.shape, 0) & (RES - 1)
    if odd:
        return jnp.where(column == 0, 0.0, pltpu.roll(values, 1, 0))
    return jnp.where(column == RES - 1, 0.0, pltpu.roll(values, values.shape[0] - 1, 0))


def column_sums(values):
    return jnp.sum(values, axis=0, keepdims=True)


def square_sums(weight_ref, out_ref):
    chans = weight_ref.shape[1]
    for start in range(0, chans, 64):
        total = None
        for tap in range(9):
            part = weight_ref[tap, pl.ds(start, 64), :].astype(jnp.float32)
            total = part * part if total is None else total + part * part
        out_ref[pl.ds(start, 64), :] = total


def demod_of(style, squares):
    spread = jnp.broadcast_to(style * style, (8, style.shape[1]))
    return lax.rsqrt(exact(spread, squares, NT)[0:1] + DEMOD_EPS)


def phase_taps(row_parity, col_parity, sign):
    found = []
    for tap, dy, dx in TAPS:
        across = col_parity + sign * dx + 2
        down = row_parity + sign * dy + 2
        copy = 1 if across in (1, 4) else 0
        phase = 2 * (down & 1) + (across & 1)
        first = PAD * (down >> 1)
        found.append((tap, phase, copy, first))
    return found


def tap_rows(ref, phase, copy, first, offset, count):
    start = first + offset
    if not isinstance(start, int):
        start = pl.multiple_of(start, PAD)
    return ref[0, phase, copy, pl.ds(start, count), :]


def write_map(ref, phase, rows_at, values, odd):
    ref[0, phase, 0, rows_at, :] = values.astype(jnp.bfloat16)
    ref[0, phase, 1, rows_at, :] = side_copy(values, odd).astype(jnp.bfloat16)


def clear_pads(ref, phase, both=True):
    empty = jnp.zeros((PAD, ref.shape[-1]), jnp.bfloat16)
    for copy in (0, 1):
        ref[0, phase, copy, 0:PAD, :] = empty
        if both:
            ref[0, phase, copy, PAD + PIX :, :] = empty


def place_of(device, shape, layout):
    across, rows, cols = layout
    row = pl.multiple_of((device // across) * rows, rows)
    col = pl.multiple_of((device % across) * cols, cols)
    return pl.ds(row, rows), pl.ds(col, cols)


def weight_copies(me, pieces, piece_refs, layout, target, sems):
    if layout is None:
        return [pltpu.make_async_copy(piece_refs[0], target, sems.at[0])]
    copies = []
    for offsets, ref in zip(pieces, piece_refs):
        for index, offset in enumerate(offsets):
            rows, cols = place_of(me ^ offset, target.shape, layout)
            copies.append(
                pltpu.make_async_copy(
                    ref.at[index], target.at[:, rows, cols], sems.at[len(copies)]
                )
            )
    return copies


def first_step():
    return (pl.program_id(0) == 0) & (pl.program_id(1) == 0)


def last_step():
    return (pl.program_id(0) == pl.num_programs(0) - 1) & (
        pl.program_id(1) == pl.num_programs(1) - 1
    )


def add_rows(total_ref, row, values):
    total_ref[row] += jnp.sum(values.reshape(values.shape[0] // 8, 8, values.shape[1]), axis=0)


def up_forward(pieces, layout, gain, waits, *refs):
    count, refs = len(pieces), refs[waits:]
    me_ref, scal_ref, feat_ref, lat_ref, small_ref, noise_ref = refs[:6]
    piece_refs = refs[6 : 6 + count]
    raw_ref, map_ref, xs_ref, sq_ref, vec_ref, whole_ref = refs[6 + count : 12 + count]
    raw_buf, weight_ref, sems, out_sem = refs[12 + count :]
    turn = pl.program_id(1)
    chans = feat_ref.shape[-1]

    @pl.when(first_step())
    def _():
        copies = weight_copies(me_ref[0], pieces, piece_refs, layout, weight_ref, sems)
        for copy in copies:
            copy.start()
        for copy in copies:
            copy.wait()
        pltpu.make_async_copy(weight_ref.at[0:9], whole_ref, out_sem).start()
        square_sums(weight_ref, sq_ref)

    @pl.when(turn == 0)
    def _():
        latent = jnp.broadcast_to(lat_ref[0], (16, lat_ref.shape[2]))
        for number in range(3):
            style = mul(latent, weight_ref[9 + number], NN)[0:1] * gain
            vec_ref[0, number : number + 1, :] = style + small_ref[number : number + 1, :]
        vec_ref[0, 3:5, :] = small_ref[3:5, :]
        vec_ref[0, 5:6, :] = demod_of(vec_ref[0, 0:1, :], sq_ref[...])
        vec_ref[0, 6:8, :] = jnp.zeros((2, chans), jnp.float32)
        style_one = vec_ref[0, 0:1, :]
        for start in range(0, PIX, TILE):
            values = feat_ref[0, pl.ds(start, TILE), :].astype(jnp.float32) * style_one
            xs_ref[0, 0, pl.ds(start, TILE), :] = values.astype(jnp.bfloat16)
            xs_ref[0, 1, pl.ds(start, TILE), :] = side_copy(values, False).astype(jnp.bfloat16)
        xs_ref[0, 0, PIX:, :] = jnp.zeros((PAD, chans), jnp.bfloat16)
        xs_ref[0, 1, PIX:, :] = jnp.zeros((PAD, chans), jnp.bfloat16)

    def one_phase(phase):
        style_two = vec_ref[0, 1:2, :]
        bias = vec_ref[0, 3:4, :]
        demod = vec_ref[0, 5:6, :]
        noise_cols = jnp.transpose(noise_ref[0, 0, phase // 2]) * scal_ref[0]
        clear_pads(map_ref, 0)

        def convolve(index):
            start = index * TILE
            raw = None
            for tap, col_step, row_step in UP_TAPS[phase]:
                part = mul(
                    xs_ref[0, col_step, pl.ds(start + PAD * row_step, TILE), :], weight_ref[tap], NT
                )
                raw = part if raw is None else raw + part
            raw_buf[index % 2] = raw

        def finish(index):
            start = index * TILE
            raw = raw_buf[index % 2]
            raw_ref[0, 0, pl.ds(start, TILE), :] = raw
            noise = noise_cols[start : start + TILE, phase % 2 : phase % 2 + 1]
            pre = raw * demod + noise + bias
            write_map(
                map_ref, 0, pl.ds(PAD + start, TILE), activate(pre) * style_two, phase % 2 == 1
            )

        steps = PIX // TILE
        for index in range(steps + 1):
            if index < steps:
                convolve(index)
            if index > 0:
                finish(index - 1)

    for phase in range(4):
        pl.when(turn == phase)(functools.partial(one_phase, phase))

    @pl.when(last_step())
    def _():
        pltpu.make_async_copy(weight_ref.at[0:9], whole_ref, out_sem).wait()


def flat_forward(pieces, layout, *refs):
    count = len(pieces)
    me_ref, scal_ref, map_ref, vec_ref, noise_ref, base_ref, mask_ref, critic_ref, rgb_ref = refs[:9]
    piece_refs = refs[9 : 9 + count]
    grad_ref, sums_ref, color_ref, whole_ref = refs[9 + count : 13 + count]
    raw_buf, sq_buf, total_buf, weight_ref, sems, out_sem = refs[13 + count :]
    row_parity = pl.program_id(1)

    @pl.when(first_step())
    def _():
        copies = weight_copies(me_ref[0], pieces, piece_refs, layout, weight_ref, sems)
        for copy in copies:
            copy.start()
        for copy in copies:
            copy.wait()
        pltpu.make_async_copy(weight_ref, whole_ref, out_sem).start()
        square_sums(weight_ref, sq_buf)

    @pl.when(row_parity == 0)
    def _():
        vec_row = demod_of(vec_ref[0, 1:2, :], sq_buf[...])
        sums_ref[0] = jnp.zeros(sums_ref.shape[1:], jnp.float32)
        sums_ref[0, 6:7, :] = vec_row
        color_ref[...] = jnp.zeros_like(color_ref)
        total_buf[...] = jnp.zeros_like(total_buf)

    style_two = vec_ref[0, 1:2, :]
    style_three = vec_ref[0, 2:3, :]
    bias = vec_ref[0, 4:5, :]
    demod = sums_ref[0, 6:7, :]
    noise_all = jnp.transpose(noise_ref[0, 0, 0])
    strength = scal_ref[1]
    rgb = rgb_ref[...]
    mix = critic_ref[...]
    out = mix[:, 4:5]
    taps = [phase_taps(row_parity, col_parity, 1) for col_parity in (0, 1)]
    per_phase = PIX // TILE
    clear_pads(grad_ref, 0)
    clear_pads(grad_ref, 1)

    def convolve(index):
        start = (index % per_phase) * TILE
        raw = None
        for tap, phase, copy, first in taps[index // per_phase]:
            part = mul(tap_rows(map_ref, phase, copy, first, start, TILE), weight_ref[tap], NT)
            raw = part if raw is None else raw + part
        raw_buf[index % 2] = raw

    def finish(index):
        col_parity = index // per_phase
        start = (index % per_phase) * TILE
        raw = raw_buf[index % 2]
        noise = noise_all[start : start + TILE, col_parity : col_parity + 1]
        pre = raw * demod + strength * noise + bias
        act = activate(pre)
        modulated = (act * style_three).astype(jnp.bfloat16)
        colors = mul(rgb, modulated, NT)[0:8] + base_ref[0, :, start : start + TILE]
        hidden = mix[:, 3:4]
        for color in range(3):
            hidden = hidden + mix[:, color : color + 1] * colors[color : color + 1]
        unit = 0.2 * hidden + 0.8 * softplus(hidden)
        logits = column_sums(out * unit)
        mask = mask_ref[0, 0, col_parity : col_parity + 1, start : start + TILE]
        grad_logits = -mask / (1.0 + jnp.exp(logits))
        grad_hidden = out * grad_logits * slope(hidden)
        grad_colors = jnp.concatenate(
            [column_sums(mix[:, color : color + 1] * grad_hidden) for color in range(3)]
            + [jnp.zeros((5, TILE), jnp.float32)],
            axis=0,
        )
        for lane in range(0, TILE, 128):
            color_ref[0] += grad_colors[:, lane : lane + 128]
        grad_low = jnp.concatenate(
            [grad_colors, jnp.zeros((8, TILE), jnp.float32)], axis=0
        ).astype(jnp.bfloat16)
        grad_map = mul(grad_low, rgb, TN)
        grad_pre = grad_map * (style_three * ROOT_TWO) * slope(pre)
        write_map(grad_ref, col_parity, pl.ds(PAD + start, TILE), grad_pre * demod, col_parity == 1)
        add_rows(total_buf, 0, grad_map * act)
        add_rows(total_buf, 1, grad_pre * raw)
        add_rows(total_buf, 2, grad_pre)
        add_rows(total_buf, 3, grad_pre * noise)
        total_buf[4] += mul(grad_low, modulated, NN)[0:8]

    steps = 2 * per_phase
    for index in range(steps + 1):
        if index < steps:
            convolve(index)
        if index > 0:
            finish(index - 1)

    @pl.when(row_parity == 1)
    def _():
        for row in range(4):
            sums_ref[0, row : row + 1, :] = column_sums(total_buf[row])
        sums_ref[0, 8:16, :] = total_buf[4]
        coef = -0.5 * demod * demod * demod * sums_ref[0, 1:2, :]
        sums_ref[0, 4:5, :] = coef
        back = exact(jnp.broadcast_to(coef, (8, coef.shape[1])), sq_buf[...], NN)[0:1]
        sums_ref[0, 5:6, :] = 2.0 * style_two * back

    @pl.when(last_step())
    def _():
        pltpu.make_async_copy(weight_ref, whole_ref, out_sem).wait()


def outer(lefts, rights):
    short = -len(lefts) % 8
    empty = [jnp.zeros((short, lefts[0].shape[1]), jnp.float32)] if short else []
    return exact(jnp.concatenate(lefts + empty), jnp.concatenate(rights + empty), TN)


def spread_out(me, order, layout, acc_ref, weight_ref, squares, out_refs):
    for tap in range(acc_ref.shape[0]):
        acc_ref[tap] += 2.0 * weight_ref[tap].astype(jnp.float32) * squares
    if layout is None:
        out_refs[0][0] = acc_ref[...].astype(out_refs[0].dtype)
        return
    for offsets, out_ref in zip(order, out_refs):
        for index, offset in enumerate(offsets):
            rows, cols = place_of(me ^ offset, acc_ref.shape, layout)
            out_ref[index] = acc_ref[:, rows, cols].astype(out_ref.dtype)


def flat_weight(order, layout, part, waits, *refs):
    me_ref, grad_ref, map_ref, weight_ref, vec_ref, sums_ref = refs[waits : waits + 6]
    out_refs, token_ref, acc_ref = refs[waits + 6 : -2], refs[-2], refs[-1]
    row_parity = pl.program_id(1)
    first = pl.multiple_of(PAD * ((row_parity + part + 1) >> 1), PAD)

    @pl.when(first_step())
    def _():
        acc_ref[...] = jnp.zeros_like(acc_ref)

    for col_parity in (0, 1):
        grad = grad_ref[0, col_parity, 0, PAD : PAD + PIX, :]
        for tap in range(3):
            across_to = col_parity + tap + 1
            copy = 1 if across_to in (1, 4) else 0
            acc_ref[tap] += mul(grad, map_ref[0, across_to & 1, copy, pl.ds(first, PIX), :], TN)

    @pl.when(last_step())
    def _():
        images = range(vec_ref.shape[0])
        squares = outer(
            [sums_ref[image, 4:5, :] for image in images],
            [vec_ref[image, 1:2, :] * vec_ref[image, 1:2, :] for image in images],
        )
        spread_out(me_ref[0], order, layout, acc_ref, weight_ref, squares, out_refs)
        token_ref[...] = squares[0:8, 0:128]


def coef_of(vec_ref, sums_ref, image):
    demod = vec_ref[image, 5:6, :]
    return -0.5 * demod * demod * demod * sums_ref[image, 1:2, :]


def up_weight(order, layout, *refs):
    me_ref, grad_ref, xs_ref, weight_ref, vec_ref, sums_ref = refs[:6]
    out_refs, acc_ref = refs[6:-1], refs[-1]

    @pl.when(pl.program_id(0) == 0)
    def _():
        acc_ref[...] = jnp.zeros_like(acc_ref)

    for phase in range(4):
        grad = grad_ref[0, phase, 0, PAD:, :]
        for tap, col_step, row_step in UP_TAPS[phase]:
            acc_ref[tap] += mul(grad, xs_ref[0, col_step, pl.ds(PAD * row_step, PIX), :], TN)

    @pl.when(pl.program_id(0) == pl.num_programs(0) - 1)
    def _():
        images = range(vec_ref.shape[0])
        squares = outer(
            [coef_of(vec_ref, sums_ref, image) for image in images],
            [vec_ref[image, 0:1, :] * vec_ref[image, 0:1, :] for image in images],
        )
        spread_out(me_ref[0], order, layout, acc_ref, weight_ref, squares, out_refs)


def flat_back(
    scal_ref, grad_ref, raw_ref, vec_ref, noise_ref, weight_ref, out_ref, sums_ref, back_buf, total_buf
):
    row_parity = pl.program_id(1)

    @pl.when(row_parity == 0)
    def _():
        total_buf[...] = jnp.zeros_like(total_buf)

    style_two = vec_ref[0, 1:2, :]
    bias = vec_ref[0, 3:4, :]
    demod = vec_ref[0, 5:6, :]
    noise_all = jnp.transpose(noise_ref[0, 0, 0])
    strength = scal_ref[0]
    taps = [phase_taps(row_parity, col_parity, -1) for col_parity in (0, 1)]
    per_phase = PIX // TILE
    clear_pads(out_ref, 0, False)
    clear_pads(out_ref, 1, False)

    def convolve(index):
        start = (index % per_phase) * TILE
        total = None
        for tap, phase, copy, first in taps[index // per_phase]:
            part = mul(tap_rows(grad_ref, phase, copy, first, start, TILE), weight_ref[tap], NN)
            total = part if total is None else total + part
        back_buf[index % 2] = total

    def finish(index):
        col_parity = index // per_phase
        start = (index % per_phase) * TILE
        grad_map = back_buf[index % 2]
        raw = raw_ref[0, col_parity, pl.ds(start, TILE), :]
        noise = noise_all[start : start + TILE, col_parity : col_parity + 1]
        pre = raw * demod + strength * noise + bias
        grad_pre = grad_map * (style_two * ROOT_TWO) * slope(pre)
        write_map(out_ref, col_parity, pl.ds(PAD + start, TILE), grad_pre * demod, col_parity == 1)
        add_rows(total_buf, 0, grad_map * activate(pre))
        add_rows(total_buf, 1, grad_pre * raw)
        add_rows(total_buf, 2, grad_pre)
        add_rows(total_buf, 3, grad_pre * noise)

    steps = 2 * per_phase
    for index in range(steps + 1):
        if index < steps:
            convolve(index)
        if index > 0:
            finish(index - 1)

    @pl.when(row_parity == 1)
    def _():
        for row in range(4):
            sums_ref[0, row : row + 1, :] = column_sums(total_buf[row])
        sums_ref[0, 4:8, :] = jnp.zeros((4, sums_ref.shape[2]), jnp.float32)


def up_back(_, grad_ref, feat_ref, vec_ref, sums_in_ref, sq_ref, weight_ref, out_ref, sums_ref):
    style_one = vec_ref[0, 0:1, :]
    total = None
    for start in range(0, PIX, TILE):
        grad_map = None
        for phase in range(4):
            for tap, col_step, row_step in UP_TAPS[phase]:
                rows = grad_ref[0, phase, col_step, pl.ds(PAD + start - PAD * row_step, TILE), :]
                part = mul(rows, weight_ref[tap], NN)
                grad_map = part if grad_map is None else grad_map + part
        found = column_sums(grad_map * feat_ref[0, pl.ds(start, TILE), :].astype(jnp.float32))
        total = found if total is None else total + found
        out_ref[0, :, pl.ds(start, TILE)] = jnp.transpose(grad_map * style_one)
    coef = coef_of(vec_ref, sums_in_ref, 0)
    back = exact(jnp.broadcast_to(coef, (8, coef.shape[1])), sq_ref[...], NN)
    sums_ref[0] = total + 2.0 * style_one * back


def small_finish(images, layout, gain, count, *refs):
    across_count, rows_own, cols_own = layout
    me_ref, row_refs = refs[0], refs[1 : 1 + count]
    old_refs = refs[1 + count : 16 + count]
    new_refs = refs[16 + count : 31 + count]
    total_ref, cross_ref = refs[31 + count :]
    device = me_ref[0]
    rows, cols = place_of(device, None, layout)
    each = total_ref.shape[0]
    stacked = jnp.concatenate([ref[...] for ref in row_refs])
    chans = stacked.shape[1]
    total_ref[...] = jnp.sum(stacked.reshape(stacked.shape[0] // each, each, chans), axis=0)
    row = lax.broadcasted_iota(jnp.int32, stacked.shape, 0) & (each - 1)
    latent_row = 3 * images
    latents = jnp.where((row >= latent_row) & (row < latent_row + images), stacked, 0.0)
    latents = latents.astype(jnp.bfloat16)

    def step(number, gradient, old=None, new=None):
        found = adam_step(*[ref[...] if old is None else ref[old] for ref in old_refs[3 * number : 3 * number + 3]], gradient, float(STEP))
        for ref, value in zip(new_refs[3 * number : 3 * number + 3], found):
            if old is None:
                ref[...] = value
            else:
                ref[old] = value

    for number in range(3):
        moved = pltpu.roll(stacked, latent_row - number * images, 0) if number < 3 else stacked
        cross_ref[...] = mul(latents, moved.astype(jnp.bfloat16), TN)
        step(0, cross_ref[rows, cols] * gain, number)
    mine = total_ref[:, cols]
    step(
        1,
        jnp.concatenate(
            [
                jnp.sum(mine[number * images : (number + 1) * images], axis=0, keepdims=True)
                for number in range(3)
            ]
        ),
    )
    first = 4 * images
    step(2, mine[first : first + 2])
    step(3, mine[first + 2 : first + 5])
    step(4, total_ref[first + 5 : first + 6, 0:5])


def call_small_finish(me, row_arrays, olds, images, layout, gain):
    chans = row_arrays[0].shape[1]
    olds = [old if old.ndim > 1 else old[None] for old in olds]
    out_shape = tuple(jax.ShapeDtypeStruct(old.shape, old.dtype) for old in olds)
    found = pl.pallas_call(
        functools.partial(small_finish, images, layout, gain, len(row_arrays)),
        in_specs=[SMEM] + [pl.BlockSpec(memory_space=pltpu.VMEM)] * (len(row_arrays) + len(olds)),
        out_specs=[pl.BlockSpec(memory_space=pltpu.VMEM)] * len(olds),
        out_shape=out_shape,
        scratch_shapes=[
            pltpu.VMEM((row_arrays[0].shape[0], chans), jnp.float32),
            pltpu.VMEM((chans, chans), jnp.float32),
        ],
        compiler_params=params(),
        name="small_finish",
    )(me, *row_arrays, *olds)
    return tuple(found[:-3]) + tuple(value[0] for value in found[-3:])


def whole(shape):
    zeros = (0,) * len(shape)
    return pl.BlockSpec(shape, lambda *ids: zeros)


def per_image(shape):
    zeros = (0,) * (len(shape) - 1)
    return pl.BlockSpec((1,) + tuple(shape[1:]), lambda image, *ids: (image,) + zeros)


SMEM = pl.BlockSpec(memory_space=pltpu.SMEM)
ANY = pl.BlockSpec(memory_space=pl.ANY)


def cost(flops, moved):
    return pl.CostEstimate(flops=int(flops), bytes_accessed=int(moved), transcendentals=0)


def half_phases(shape, count=2):
    zeros = (0,) * (len(shape) - 2)
    return pl.BlockSpec(
        (1, count) + tuple(shape[2:]), lambda image, turn: (image, turn) + zeros
    )


def noise_spec(layer):
    return pl.BlockSpec((1, 1, 1, 8, PIX), lambda image, parity: (image, layer, parity, 0, 0))


def offsets_of(weight):
    return tuple(offsets for offsets, _ in weight[0])


def call_up_forward(after, me, scalars, feat, lat, small, noise, weight):
    images, _, chans = feat.shape
    arrays, layout = [array for _, array in weight[0]], weight[1]
    out_shape = (
        jax.ShapeDtypeStruct((images, 4, PIX, chans), jnp.float32),
        jax.ShapeDtypeStruct((images, 4, 2, ROWS, chans), jnp.bfloat16),
        jax.ShapeDtypeStruct((images, 2, PIX + PAD, chans), jnp.bfloat16),
        jax.ShapeDtypeStruct((chans, chans), jnp.float32),
        jax.ShapeDtypeStruct((images, 8, chans), jnp.float32),
        jax.ShapeDtypeStruct((9, chans, chans), jnp.bfloat16),
    )
    return pl.pallas_call(
        functools.partial(
            up_forward, offsets_of(weight), layout, lat.shape[2] ** (-0.5), len(after)
        ),
        grid=(images, 4),
        in_specs=[ANY] * len(after)
        + [
            SMEM,
            SMEM,
            per_image(feat.shape),
            per_image(lat.shape),
            whole(small.shape),
            pl.BlockSpec((1, 1, 2, 8, PIX), lambda image, turn: (image, 0, 0, 0, 0)),
        ]
        + [ANY] * len(arrays),
        out_specs=[
            half_phases(out_shape[0].shape, 1),
            half_phases(out_shape[1].shape, 1),
            per_image(out_shape[2].shape),
            whole(out_shape[3].shape),
            per_image(out_shape[4].shape),
            ANY,
        ],
        out_shape=out_shape,
        scratch_shapes=[
            pltpu.VMEM((2, TILE, chans), jnp.float32),
            pltpu.VMEM((12, chans, chans), jnp.bfloat16),
            pltpu.SemaphoreType.DMA((sum(len(o) for o in offsets_of(weight)),)),
            pltpu.SemaphoreType.DMA,
        ],
        compiler_params=params(),
        cost_estimate=cost(18 * images * PIX * chans * chans, 60e6),
        name="up_forward",
    )(*after, me, scalars, feat, lat, small, noise, *arrays)


def call_flat_forward(me, scalars, maps, vecs, noise, base, mask, critic, rgb, weight):
    images, chans = maps.shape[0], maps.shape[-1]
    arrays, layout = [array for _, array in weight[0]], weight[1]
    out_shape = (
        jax.ShapeDtypeStruct((images, 4, 2, ROWS, chans), jnp.bfloat16),
        jax.ShapeDtypeStruct((images, 16, chans), jnp.float32),
        jax.ShapeDtypeStruct((images, 8, 128), jnp.float32),
        jax.ShapeDtypeStruct((9, chans, chans), jnp.bfloat16),
    )
    return pl.pallas_call(
        functools.partial(flat_forward, offsets_of(weight), layout),
        grid=(images, 2),
        in_specs=[
            SMEM,
            SMEM,
            per_image(maps.shape),
            per_image(vecs.shape),
            noise_spec(1),
            per_image(base.shape),
            pl.BlockSpec((1, 1, 8, PIX), lambda image, parity: (image, parity, 0, 0)),
            whole(critic.shape),
            whole(rgb.shape),
        ]
        + [ANY] * len(arrays),
        out_specs=[
            half_phases(out_shape[0].shape),
            per_image(out_shape[1].shape),
            per_image(out_shape[2].shape),
            ANY,
        ],
        out_shape=out_shape,
        scratch_shapes=[
            pltpu.VMEM((2, TILE, chans), jnp.float32),
            pltpu.VMEM((chans, chans), jnp.float32),
            pltpu.VMEM((5, 8, chans), jnp.float32),
            pltpu.VMEM((9, chans, chans), jnp.bfloat16),
            pltpu.SemaphoreType.DMA((sum(len(o) for o in offsets_of(weight)),)),
            pltpu.SemaphoreType.DMA,
        ],
        compiler_params=params(),
        cost_estimate=cost(72 * images * PIX * chans * chans, 60e6),
        name="flat_forward",
    )(me, scalars, maps, vecs, noise, base, mask, critic, rgb, *arrays)


def gradient_shapes(chans, taps, layout):
    if layout is None:
        return (jax.ShapeDtypeStruct((1, taps, chans, chans), jnp.float32),)
    _, rows, cols = layout
    shape = (16, taps, rows, cols)
    return (jax.ShapeDtypeStruct(shape, jnp.float32), jax.ShapeDtypeStruct(shape, jnp.bfloat16))


def call_flat_weight(me, after, grad, maps, weight, vecs, sums, order, layout, part):
    images, chans = maps.shape[0], maps.shape[-1]
    out_shape = gradient_shapes(chans, 3, layout) + (jax.ShapeDtypeStruct((8, 128), jnp.float32),)
    return pl.pallas_call(
        functools.partial(flat_weight, order, layout, part, len(after)),
        grid=(images, 2),
        in_specs=[ANY] * len(after)
        + [
            SMEM,
            pl.BlockSpec((1, 2, 1, ROWS, chans), lambda image, parity: (image, parity, 0, 0, 0)),
            pl.BlockSpec(
                (1, 2, 2, ROWS, chans), lambda image, parity: (image, (parity + part + 1) & 1, 0, 0, 0)
            ),
            pl.BlockSpec((3, chans, chans), lambda image, parity: (part, 0, 0)),
            whole(vecs.shape),
            whole(sums.shape),
        ],
        out_specs=[whole(s.shape) for s in out_shape],
        out_shape=out_shape,
        scratch_shapes=[pltpu.VMEM((3, chans, chans), jnp.float32)],
        compiler_params=params(),
        cost_estimate=cost(24 * images * PIX * chans * chans, 40e6),
        name="flat_weight_" + str(part),
    )(*after, me, grad, maps, weight, vecs, sums)


def call_flat_back(scalars, grad, raw, vecs, noise, weight):
    images, chans = grad.shape[0], grad.shape[-1]
    out_shape = (
        jax.ShapeDtypeStruct((images, 4, 2, PIX + PAD, chans), jnp.bfloat16),
        jax.ShapeDtypeStruct((images, 8, chans), jnp.float32),
    )
    return pl.pallas_call(
        flat_back,
        grid=(images, 2),
        in_specs=[
            SMEM,
            per_image(grad.shape),
            half_phases(raw.shape),
            per_image(vecs.shape),
            noise_spec(0),
            whole(weight.shape),
        ],
        out_specs=[half_phases(out_shape[0].shape), per_image(out_shape[1].shape)],
        out_shape=out_shape,
        scratch_shapes=[
            pltpu.VMEM((2, TILE, chans), jnp.float32),
            pltpu.VMEM((4, 8, chans), jnp.float32),
        ],
        compiler_params=params(),
        cost_estimate=cost(72 * images * PIX * chans * chans, 60e6),
        name="flat_back",
    )(scalars, grad, raw, vecs, noise, weight)


def call_up_weight(me, grad, xs, weight, vecs, sums, order, layout):
    images, chans = xs.shape[0], xs.shape[-1]
    out_shape = gradient_shapes(chans, 9, layout)
    return pl.pallas_call(
        functools.partial(up_weight, order, layout),
        grid=(images,),
        in_specs=[
            SMEM,
            pl.BlockSpec((1, 4, 1, PIX + PAD, chans), lambda image: (image, 0, 0, 0, 0)),
            per_image(xs.shape),
            whole(weight.shape),
            whole(vecs.shape),
            whole(sums.shape),
        ],
        out_specs=[whole(s.shape) for s in out_shape],
        out_shape=out_shape,
        scratch_shapes=[pltpu.VMEM((9, chans, chans), jnp.float32)],
        compiler_params=params(),
        cost_estimate=cost(18 * images * PIX * chans * chans, 30e6),
        name="up_weight",
    )(me, grad, xs, weight, vecs, sums)


def call_up_back(after, grad, feat, vecs, sums, squares, weight):
    images, _, chans = feat.shape
    out_shape = (
        jax.ShapeDtypeStruct((images, chans, PIX), jnp.float32),
        jax.ShapeDtypeStruct((images, 8, chans), jnp.float32),
    )
    return pl.pallas_call(
        up_back,
        grid=(images,),
        in_specs=[
            ANY,
            per_image(grad.shape),
            per_image(feat.shape),
            per_image(vecs.shape),
            per_image(sums.shape),
            whole(squares.shape),
            whole(weight.shape),
        ],
        out_specs=[per_image(out_shape[0].shape), per_image(out_shape[1].shape)],
        out_shape=out_shape,
        compiler_params=params(),
        cost_estimate=cost(18 * images * PIX * chans * chans, 30e6),
        name="up_back",
    )(after, grad, feat, vecs, sums, squares, weight)


BIT_X, BIT_CORE, BIT_Y, BIT_LOW, BIT_HIGH = 1, 2, 4, 8, 16
Z_OFFSETS = ((0, BIT_LOW), (BIT_HIGH, BIT_HIGH + BIT_LOW))


def across(values, bits, devices):
    return lax.ppermute(values, BOTH, [(device, device ^ bits) for device in range(devices)])


def gather_along_z(block, devices):
    move = lambda values, bits: across(values, bits, devices)
    low = jnp.stack([block, move(block, BIT_LOW)])
    return low, jnp.stack([move(block, BIT_HIGH), move(block, BIT_HIGH + BIT_LOW)])


def gather_in_turn(low, high, devices, ahead):
    move = lambda values, bits: across(values, bits, devices)
    high_y, low_y = move(high, BIT_Y), move(low, BIT_Y)
    low_ahead, high_ahead, _ = lax.optimization_barrier((low, high, ahead))
    low_x, high_x = move(low_ahead, BIT_X), move(high_ahead, BIT_X)
    low_xy, high_xy = move(low_x, BIT_Y), move(high_y, BIT_X)
    found = []
    for offsets, arrays in zip(
        Z_OFFSETS, ((low, low_x, low_y, low_xy), (high, high_x, high_y, high_xy))
    ):
        for bits, array in zip((0, BIT_X, BIT_Y, BIT_X + BIT_Y), arrays):
            found.append((tuple(o ^ bits for o in offsets), array))
    return found


def gather_at_once(along, devices):
    found = []
    offsets = Z_OFFSETS[0] + Z_OFFSETS[1]
    for bits in (0, BIT_X + BIT_Y, BIT_X, BIT_Y):
        array = across(along, bits, devices) if bits else along
        found.append((tuple(o ^ bits for o in offsets), array))
    return found


def with_other_core(found, devices):
    return found + [
        (tuple(o ^ BIT_CORE for o in offsets), across(array, BIT_CORE, devices))
        for offsets, array in found
    ]


def tie(values, token):
    return values if token is None else lax.optimization_barrier((values, token))[0]


def gather_rows(rows, devices):
    move = lambda values, bits: across(values, bits, devices)
    token = yield (rows,)
    found = [rows] + tie([move(rows, b) for b in (BIT_LOW, BIT_HIGH, BIT_LOW + BIT_HIGH)], token)
    for bits in (BIT_X, BIT_Y, BIT_CORE):
        joined = jnp.concatenate(found)
        token = yield (joined,)
        found = found + tie([move(joined, bits)], token)
    yield found


def scatter_order():
    kept = []
    for high in (0, 1):
        one, two = (BIT_X, BIT_Y) if high == 0 else (BIT_Y, BIT_X)
        for a in (0, 1):
            for b in (0, 1):
                for low in (0, 1):
                    kept.append(high * BIT_HIGH + low * BIT_LOW + a * one + b * two)
    return tuple(kept), tuple(offset ^ BIT_CORE for offset in kept)


def scatter_blocks(kept, sent, devices):
    low = lambda values: values.astype(jnp.bfloat16)

    def swap(values, bits, token):
        found = tie([across(v, b, devices) for v, b in zip(values, bits)], token)
        return [f.astype(jnp.float32) for f in found]

    token = yield (sent,)
    total = kept + swap((sent,), (BIT_CORE,), token)[0]
    total = total.reshape((2, 2, 2, 2) + kept.shape[1:])
    sends = low(total[0, 1]), low(total[1, 1])
    token = yield sends
    found = swap(sends, (BIT_X, BIT_Y), token)
    halves = total[0, 0] + found[0], total[1, 0] + found[1]
    sends = low(halves[0][1]), low(halves[1][1])
    token = yield sends
    found = swap(sends, (BIT_Y, BIT_X), token)
    halves = halves[0][0] + found[0], halves[1][0] + found[1]
    sends = low(halves[0][1]), low(halves[1][0]), low(halves[1][1])
    token = yield sends
    total = halves[0][0]
    for found in swap(sends, (BIT_LOW, BIT_HIGH, BIT_HIGH + BIT_LOW), token):
        total = total + found
    yield total


def gather_whole(block, n_img, n_ch):
    _, rows, cols = block.shape
    every = lax.all_gather(block, BOTH, axis=0, tiled=False)
    every = every.reshape(n_img, n_ch, -1, rows, cols)
    return jnp.transpose(every, (2, 0, 3, 1, 4)).reshape(-1, n_img * rows, n_ch * cols)


def scatter_whole(grad, n_img, n_ch, rows, cols):
    grad = grad.reshape(-1, n_img, rows, n_ch, cols)
    grad = jnp.transpose(grad, (1, 3, 0, 2, 4)).reshape(n_img * n_ch, -1, rows, cols)
    return lax.psum_scatter(grad, BOTH, scatter_dimension=0, tiled=False)


def adam_step(weight, mean_old, square_old, gradient, count):
    moment = BETA_ONE * mean_old + (1.0 - BETA_ONE) * gradient
    variance = BETA_TWO * square_old + (1.0 - BETA_TWO) * gradient * gradient
    fix_one = 1.0 - BETA_ONE**count
    fix_two = 1.0 - BETA_TWO**count
    update = moment / fix_one / (jnp.sqrt(variance / fix_two) + ADAM_EPS) + DECAY_RATE * weight
    return (weight - LEARN_RATE * update, moment, variance)


def phases_of_lanes(side):
    column = jnp.arange(side, dtype=jnp.int32)
    target = (column % 2) * (side // 2) + column // 2
    return (target[:, None] == column[None, :]).astype(jnp.float32)


def padded(values, rows):
    short = rows - values.shape[-2]
    shape = values.shape[:-2] + (short, values.shape[-1])
    return jnp.concatenate([values, jnp.zeros(shape, values.dtype)], axis=-2)


def body(
    n_img,
    n_ch,
    features,
    latents,
    skip_rgb,
    noises,
    ada_shift,
    crop_mask,
    critic_mix,
    critic_bias,
    critic_out,
    upsampler,
    upsampler_mean,
    upsampler_square,
    refiner,
    refiner_mean,
    refiner_square,
    affines,
    affines_mean,
    affines_square,
    modbias,
    modbias_mean,
    modbias_square,
    actbias,
    actbias_mean,
    actbias_square,
    rgbmix,
    rgbmix_mean,
    rgbmix_square,
    scalars,
    scalars_mean,
    scalars_square,
):
    local_chans, group_images = features.shape[0], features.shape[1]
    chans = local_chans * n_ch
    rows_own = upsampler.shape[2]
    side = 2 * RES
    devices = n_img * n_ch
    by_hand = devices == 32 and n_ch == 2 and group_images % n_ch == 0
    share = max(1, n_ch // group_images)
    images = group_images * share // n_ch
    ch_index = lax.axis_index("ch")
    img_index = lax.axis_index("img")
    me = (img_index * n_ch + ch_index).astype(jnp.int32)[None]
    first = (ch_index // share) * images
    col_start = ch_index * local_chans

    def mine(values, axis):
        return lax.dynamic_slice_in_dim(values, first, images, axis)

    def my_chans(values, axis):
        return lax.dynamic_slice_in_dim(values, col_start, local_chans, axis)

    up_block = jnp.concatenate([jnp.transpose(upsampler, (1, 2, 0)), affines]).astype(jnp.bfloat16)
    ref_block = jnp.transpose(refiner, (1, 2, 0)).astype(jnp.bfloat16)
    small_own = jnp.concatenate([modbias, actbias, rgbmix], axis=0)
    if by_hand:
        layout, order = (n_ch, rows_own, local_chans), scatter_order()
        other = lax.dynamic_slice_in_dim(features, images - first, images, 1)
        other = across(other, BIT_X, devices)
        up_low, up_high = gather_along_z(up_block, devices)
        ref_along = jnp.concatenate(gather_along_z(ref_block, devices))
        up_weight_all = (
            with_other_core(gather_in_turn(up_low, up_high, devices, other), devices), layout
        )
        here = mine(features, 1)
        feat = jnp.where(
            ch_index == 0, jnp.concatenate([here, other]), jnp.concatenate([other, here])
        )
        small_other = across(small_own, BIT_X, devices)
        small = jnp.where(
            ch_index == 0,
            jnp.concatenate([small_own, small_other], axis=1),
            jnp.concatenate([small_other, small_own], axis=1),
        )
        ref_plane = gather_at_once(ref_along, devices)
        ahead = (ref_along,)
    else:
        layout, order, ahead = None, None, ()
        up_weight_all = ([((0,), gather_whole(up_block, n_img, n_ch))], None)
        ref_weight_all = ([((0,), gather_whole(ref_block, n_img, n_ch))], None)
        small = lax.all_gather(small_own, "ch", axis=1, tiled=True)
        feat = mine(lax.all_gather(features, "ch", axis=0, tiled=True), 1)
    feat = jnp.transpose(feat, (1, 2, 0))
    lat_own = mine(latents, 0)
    rgb_low = padded(small[5:8] * C ** (-0.5), 16).astype(jnp.bfloat16)
    noise = jnp.dot(
        mine(noises, 1).reshape(2 * images * side, side), phases_of_lanes(side), precision=PRECISE
    )
    noise = jnp.transpose(noise.reshape(2, images, RES, 2, 2, RES), (1, 0, 3, 4, 2, 5))
    noise = padded(noise.reshape(images, 2, 2, 2, PIX), 8)
    order_in = jnp.arange(side, dtype=jnp.int32)
    order_in = 2 * (order_in % RES) + order_in // RES
    shifts = mine(ada_shift, 0)
    picks = [
        (((order_in[None, :] + shifts[:, axis : axis + 1]) % side)[:, :, None] == jnp.arange(side)).astype(
            jnp.bfloat16
        )
        for axis in (0, 1)
    ]
    mask = mine(crop_mask, 0).reshape(images, side, side).astype(jnp.bfloat16)
    mask = jnp.einsum("byz,bzx->byx", picks[0], mask, preferred_element_type=jnp.bfloat16)
    mask = jnp.einsum("byx,bwx->byw", mask, picks[1], preferred_element_type=jnp.float32) / share
    mask = jnp.transpose(mask.reshape(images, 2, RES, 2, RES), (0, 1, 3, 2, 4))
    mask = padded(mask.reshape(images, 2, 2, PIX), 8)
    base = padded(
        jnp.transpose(mine(skip_rgb, 1), (1, 0, 2)) + scalars[2:5][None, :, None], 8
    )
    critic = jnp.concatenate(
        [critic_mix, critic_bias[:, None], critic_out[:, None], jnp.zeros((critic_mix.shape[0], 3))], axis=1
    )

    raw_one, maps, xs, up_square, vecs, up_full = call_up_forward(
        ahead, me, scalars, feat, lat_own[:, None, :], small, noise, up_weight_all
    )
    if by_hand:
        arrays, _ = lax.optimization_barrier(([array for _, array in ref_plane], vecs))
        ref_plane = [(offsets, array) for (offsets, _), array in zip(ref_plane, arrays)]
        ref_weight_all = (with_other_core(ref_plane, devices), layout)
    grad_two, sums_two, color_sums, ref_full = call_flat_forward(
        me, scalars, maps, vecs, noise, base, mask, critic, rgb_low, ref_weight_all
    )
    grad_one, sums_one = call_flat_back(scalars, grad_two, raw_one, vecs, noise, ref_full)
    up_parts = call_up_weight(me, grad_one, xs, up_full, vecs, sums_one, order, layout)
    feat_grad, feat_sums = call_up_back(
        up_parts[0], grad_one, feat, vecs, sums_one, up_square, up_full
    )

    style_grads = jnp.stack(
        [feat_sums[:, 0], sums_one[:, 0] + sums_two[:, 5], sums_two[:, 0]]
    )
    style_grads = style_grads.astype(jnp.bfloat16).astype(jnp.float32)
    color_sum = jnp.sum(color_sums[:, 0:3], axis=(0, 2))
    scalar_row = jnp.concatenate(
        [
            jnp.sum(sums_one[:, 3])[None],
            jnp.sum(sums_two[:, 3])[None],
            color_sum,
            jnp.zeros((chans - 5,), jnp.float32),
        ]
    )
    packed = jnp.concatenate(
        [
            style_grads.reshape(3 * images, chans),
            lat_own.astype(jnp.float32),
            jnp.sum(sums_one[:, 2], axis=0)[None],
            jnp.sum(sums_two[:, 2], axis=0)[None],
            jnp.sum(sums_two[:, 8:11], axis=0) * C ** (-0.5),
            scalar_row[None],
        ],
        axis=0,
    )
    packed = padded(packed, 16)

    def ref_part(after, part):
        return call_flat_weight(
            me, after, grad_two, maps, ref_full, vecs, sums_two, order, layout, part
        )

    if by_hand:
        other = lax.dynamic_slice_in_dim(feat_grad, local_chans - col_start, local_chans, 1)
        other = other.astype(jnp.bfloat16)
        row_steps = gather_rows(packed, devices)
        up_steps = scatter_blocks(*up_parts, devices)
        next(up_steps)
        kept, sent, token = ref_part(up_steps.send(feat_sums) + next(row_steps) + (other,), 0)
        other = tie(across(other, BIT_X, devices), token)
        steps = [scatter_blocks(kept, sent, devices)]
        next(steps[0])
        kept, sent, token = ref_part(up_steps.send(token) + row_steps.send(token) + (token,), 1)
        steps.append(scatter_blocks(kept, sent, devices))
        next(steps[1])
        kept, sent, token = ref_part(
            up_steps.send(token) + steps[0].send(token) + row_steps.send(token) + (token,), 2
        )
        steps.append(scatter_blocks(kept, sent, devices))
        up_grad = up_steps.send(token)
        row_steps.send(token)
        all_rows = next(row_steps)
        steps[0].send(token)
        next(steps[1])
        ref_grad = jnp.concatenate([list(step)[-1] for step in steps])
    else:
        up_grad = scatter_whole(up_parts[0], n_img, n_ch, rows_own, local_chans)
        ref_grad = jnp.concatenate(
            [
                scatter_whole(ref_part((), part)[0], n_img, n_ch, rows_own, local_chans)
                for part in range(3)
            ]
        )
    up_grad = jnp.transpose(up_grad, (2, 0, 1))
    ref_grad = jnp.transpose(ref_grad, (2, 0, 1))

    if by_hand:
        kept = my_chans(feat_grad, 1)
        other = other.astype(jnp.float32)
        feat_grad = jnp.where(
            ch_index == 0, jnp.concatenate([kept, other]), jnp.concatenate([other, kept])
        )
    else:
        feat_grad = lax.all_gather(feat_grad, "ch", axis=0, tiled=True)[::share] * share
        feat_grad = my_chans(feat_grad, 1)
    features_grad = jnp.transpose(feat_grad, (1, 0, 2))

    count = float(STEP)
    style_gain = latents.shape[1] ** (-0.5)
    small_old = (
        affines,
        affines_mean,
        affines_square,
        modbias,
        modbias_mean,
        modbias_square,
        actbias,
        actbias_mean,
        actbias_square,
        rgbmix,
        rgbmix_mean,
        rgbmix_square,
        scalars,
        scalars_mean,
        scalars_square,
    )
    if by_hand:
        small_new = call_small_finish(
            me, all_rows, small_old, images, layout, style_gain
        )
    else:
        every = lax.all_gather(packed, BOTH, axis=0, tiled=False)
        first_sum = 4 * images
        sums = jnp.sum(every[:, first_sum : first_sum + 6], axis=0)
        lat_rows = affines.shape[1]
        lat_cols = every[:, 3 * images : first_sum]
        lat_cols = lax.dynamic_slice_in_dim(lat_cols, img_index * lat_rows, lat_rows, 2)
        style_all = my_chans(every[:, : 3 * images], 2)
        style_all = style_all.reshape(devices, 3, images, local_chans)
        aff_grad = style_gain * jnp.einsum(
            "dbj,dkbi->kji",
            lat_cols.astype(jnp.bfloat16),
            style_all.astype(jnp.bfloat16),
            preferred_element_type=jnp.float32,
        )
        small_grad = my_chans(sums[0:5], 1)
        small_new = ()
        for number, gradient in enumerate(
            (aff_grad, jnp.sum(style_all, axis=(0, 2)), small_grad[0:2], small_grad[2:5], sums[5, 0:5])
        ):
            small_new += adam_step(*small_old[3 * number : 3 * number + 3], gradient, count)

    up_new = adam_step(upsampler, upsampler_mean, upsampler_square, up_grad, count)
    ref_new = adam_step(refiner, refiner_mean, refiner_square, ref_grad, count)
    return (features_grad,) + up_new + ref_new + tuple(small_new)


def solution(mesh):
    conv = P("ch", None, "img")
    aff = P(None, "img", "ch")
    row = P(None, "ch")
    images = P(None, "img", None)
    return jax.shard_map(
        functools.partial(body, mesh.shape["img"], mesh.shape["ch"]),
        mesh=mesh,
        in_specs=(P("ch", "img", None), P("img", None), images, images, P("img", None), P("img", None))
        + (P(),) * 3
        + (conv,) * 6
        + (aff,) * 3
        + (row,) * 9
        + (P(),) * 3,
        out_specs=(P("ch", "img", None),) + (conv,) * 6 + (aff,) * 3 + (row,) * 9 + (P(),) * 3,
        check_vma=False,
    )
```

```python
import functools

import jax
import jax.numpy as jnp
from jax import lax
from jax.experimental import pallas as pl
from jax.experimental.pallas import tpu as pltpu
from jax.sharding import PartitionSpec as P

C = 512
RES = 32
STEP = 10

PRECISE = lax.Precision.HIGHEST
ROOT_TWO = 1.4142135623730951
LOG_TWO = 0.6931471805599453
BETA_ONE = 0.9
BETA_TWO = 0.99
LEARN_RATE = 0.3
DECAY_RATE = 0.01
ADAM_EPS = 1e-08
DEMOD_EPS = 1e-08
VMEM_LIMIT = 60 * 2**20
BOTH = ("img", "ch")

PAD = RES
PIX = RES * RES
ROWS = PIX + 2 * PAD
TILE = 256
TAPS = tuple((3 * (dy + 1) + dx + 1, dy, dx) for dy in (-1, 0, 1) for dx in (-1, 0, 1))
UP_TAPS = (
    ((4, 0, 0),),
    ((3, 0, 0), (5, 1, 0)),
    ((1, 0, 0), (7, 0, 1)),
    ((0, 0, 0), (2, 1, 0), (6, 0, 1), (8, 1, 1)),
)
NT = (((1,), (1,)), ((), ()))
TN = (((0,), (0,)), ((), ()))
NN = (((1,), (0,)), ((), ()))


def params(**more):
    return pltpu.CompilerParams(vmem_limit_bytes=VMEM_LIMIT, **more)


def mul(left, right, dims):
    return lax.dot_general(left, right, dims, preferred_element_type=jnp.float32)


def exact(left, right, dims):
    return lax.dot_general(
        left, right, dims, precision=PRECISE, preferred_element_type=jnp.float32
    )


def half_tanh(values):
    return jnp.tanh(0.5 * values)


def leaky(values, half, scale):
    line = (0.6 * scale) * values + (0.4 * scale) * jnp.abs(values)
    return line + ((0.8 * scale * LOG_TWO) - (0.8 * scale) * jnp.log(1.0 + jnp.abs(half)))


def slope(half):
    return 0.6 + 0.4 * half


def slope_of(style, half):
    return (0.6 * ROOT_TWO) * style + ((0.4 * ROOT_TWO) * style) * half


def side_copy(values, odd):
    column = lax.broadcasted_iota(jnp.int32, values.shape, 0) & (RES - 1)
    if odd:
        return jnp.where(column == 0, 0.0, pltpu.roll(values, 1, 0))
    return jnp.where(column == RES - 1, 0.0, pltpu.roll(values, values.shape[0] - 1, 0))


def column_sums(values):
    return jnp.sum(values, axis=0, keepdims=True)


def square_sums(weight_ref, out_ref):
    chans = weight_ref.shape[1]
    for start in range(0, chans, 64):
        total = None
        for tap in range(9):
            part = weight_ref[tap, pl.ds(start, 64), :].astype(jnp.float32)
            total = part * part if total is None else total + part * part
        out_ref[pl.ds(start, 64), :] = total


def demod_of(style, squares):
    spread = jnp.broadcast_to(style * style, (8, style.shape[1]))
    return lax.rsqrt(exact(spread, squares, NT)[0:1] + DEMOD_EPS)


def phase_taps(row_parity, col_parity, sign):
    found = []
    for tap, dy, dx in TAPS:
        across = col_parity + sign * dx + 2
        down = row_parity + sign * dy + 2
        copy = 1 if across in (1, 4) else 0
        phase = 2 * (down & 1) + (across & 1)
        first = PAD * (down >> 1)
        found.append((tap, phase, copy, first))
    return found


def tap_rows(ref, phase, copy, first, offset, count):
    start = first + offset
    if not isinstance(start, int):
        start = pl.multiple_of(start, PAD)
    return ref[0, phase, copy, pl.ds(start, count), :]


def write_map(ref, phase, rows_at, values, odd):
    ref[0, phase, 0, rows_at, :] = values.astype(jnp.bfloat16)
    ref[0, phase, 1, rows_at, :] = side_copy(values, odd).astype(jnp.bfloat16)


def clear_pads(ref, phase, both=True):
    empty = jnp.zeros((PAD, ref.shape[-1]), jnp.bfloat16)
    for copy in (0, 1):
        ref[0, phase, copy, 0:PAD, :] = empty
        if both:
            ref[0, phase, copy, PAD + PIX :, :] = empty


def place_of(device, layout):
    across, rows, cols = layout
    row = pl.multiple_of((device // across) * rows, rows)
    col = pl.multiple_of((device % across) * cols, cols)
    return pl.ds(row, rows), pl.ds(col, cols)


def weight_copies(me, pieces, piece_refs, layout, target, sems):
    if layout is None:
        return [pltpu.make_async_copy(piece_refs[0], target, sems.at[0])]
    copies = []
    for offsets, ref in zip(pieces, piece_refs):
        for index, offset in enumerate(offsets):
            rows, cols = place_of(me ^ offset, layout)
            copies.append(
                pltpu.make_async_copy(
                    ref.at[index], target.at[:, rows, cols], sems.at[len(copies)]
                )
            )
    return copies


def transpose_taps(weight_ref, out_ref):
    for tap in range(9):
        out_ref[tap] = jnp.transpose(weight_ref[tap])


def first_step():
    return (pl.program_id(0) == 0) & (pl.program_id(1) == 0)


def last_step():
    return (pl.program_id(0) == pl.num_programs(0) - 1) & (
        pl.program_id(1) == pl.num_programs(1) - 1
    )


def add_rows(total_ref, row, values):
    total_ref[row] += jnp.sum(values.reshape(values.shape[0] // 8, 8, values.shape[1]), axis=0)


def up_forward(pieces, layout, gain, waits, *refs):
    count, refs = len(pieces), refs[waits:]
    me_ref, scal_ref, feat_ref, lat_ref, small_ref, noise_ref = refs[:6]
    piece_refs = refs[6 : 6 + count]
    raw_ref, map_ref, xs_ref, sq_ref, vec_ref, whole_ref = refs[6 + count : 12 + count]
    raw_buf, weight_ref, sems, out_sem = refs[12 + count :]
    turn = pl.program_id(1)
    chans = feat_ref.shape[-1]

    @pl.when(first_step())
    def _():
        copies = weight_copies(me_ref[0], pieces, piece_refs, layout, weight_ref, sems)
        for copy in copies:
            copy.start()
        for copy in copies:
            copy.wait()
        pltpu.make_async_copy(weight_ref.at[0:9], whole_ref, out_sem).start()
        square_sums(weight_ref, sq_ref)

    @pl.when(turn == 0)
    def _():
        latent = jnp.broadcast_to(lat_ref[0], (16, lat_ref.shape[2]))
        for number in range(3):
            style = mul(latent, weight_ref[9 + number], NN)[0:1] * gain
            vec_ref[0, number : number + 1, :] = style + small_ref[number : number + 1, :]
        vec_ref[0, 3:5, :] = small_ref[3:5, :]
        vec_ref[0, 5:6, :] = demod_of(vec_ref[0, 0:1, :], sq_ref[...])
        vec_ref[0, 6:8, :] = jnp.zeros((2, chans), jnp.float32)
        style_one = vec_ref[0, 0:1, :]
        for start in range(0, PIX, TILE):
            values = feat_ref[0, pl.ds(start, TILE), :].astype(jnp.float32) * style_one
            xs_ref[0, 0, pl.ds(start, TILE), :] = values.astype(jnp.bfloat16)
            xs_ref[0, 1, pl.ds(start, TILE), :] = side_copy(values, False).astype(jnp.bfloat16)
        xs_ref[0, 0, PIX:, :] = jnp.zeros((PAD, chans), jnp.bfloat16)
        xs_ref[0, 1, PIX:, :] = jnp.zeros((PAD, chans), jnp.bfloat16)

    def one_phase(phase):
        style_two = vec_ref[0, 1:2, :]
        bias = vec_ref[0, 3:4, :]
        demod = vec_ref[0, 5:6, :]
        noise_cols = jnp.transpose(noise_ref[0, 0, phase // 2]) * scal_ref[0]
        clear_pads(map_ref, 0)

        def convolve(index):
            start = index * TILE
            raw = None
            for tap, col_step, row_step in UP_TAPS[phase]:
                part = mul(
                    xs_ref[0, col_step, pl.ds(start + PAD * row_step, TILE), :], weight_ref[tap], NT
                )
                raw = part if raw is None else raw + part
            raw_buf[index % 2] = raw

        def finish(index):
            start = index * TILE
            raw = raw_buf[index % 2]
            raw_ref[0, 0, pl.ds(start, TILE), :] = raw
            noise = noise_cols[start : start + TILE, phase % 2 : phase % 2 + 1]
            pre = raw * demod + (noise + bias)
            act = leaky(pre, half_tanh(pre), ROOT_TWO)
            write_map(
                map_ref, 0, pl.ds(PAD + start, TILE), act * style_two, phase % 2 == 1
            )

        steps = PIX // TILE
        for index in range(steps + 1):
            if index < steps:
                convolve(index)
            if index > 0:
                finish(index - 1)

    for phase in range(4):
        pl.when(turn == phase)(functools.partial(one_phase, phase))

    @pl.when(last_step())
    def _():
        pltpu.make_async_copy(weight_ref.at[0:9], whole_ref, out_sem).wait()


def flat_forward(pieces, layout, *refs):
    count = len(pieces)
    me_ref, scal_ref, map_ref, vec_ref, noise_ref, base_ref, mask_ref, critic_ref, rgb_ref, rgb_cols_ref = refs[:10]
    piece_refs = refs[10 : 10 + count]
    grad_ref, sums_ref, color_ref, whole_ref = refs[10 + count : 14 + count]
    raw_buf, act_buf, half_buf, low_buf, turned_ref, sq_buf, total_buf, weight_ref, sems, out_sem = refs[
        14 + count :
    ]
    row_parity = pl.program_id(1)

    @pl.when(first_step())
    def _():
        copies = weight_copies(me_ref[0], pieces, piece_refs, layout, weight_ref, sems)
        for copy in copies:
            copy.start()
        for copy in copies:
            copy.wait()
        pltpu.make_async_copy(weight_ref, whole_ref, out_sem).start()
        transpose_taps(weight_ref, turned_ref)
        square_sums(weight_ref, sq_buf)

    @pl.when(row_parity == 0)
    def _():
        vec_row = demod_of(vec_ref[0, 1:2, :], sq_buf[...])
        sums_ref[0] = jnp.zeros(sums_ref.shape[1:], jnp.float32)
        sums_ref[0, 6:7, :] = vec_row
        color_ref[...] = jnp.zeros_like(color_ref)
        total_buf[...] = jnp.zeros_like(total_buf)

    style_two = vec_ref[0, 1:2, :]
    style_three = vec_ref[0, 2:3, :]
    bias = vec_ref[0, 4:5, :]
    demod = sums_ref[0, 6:7, :]
    noise_all = jnp.transpose(noise_ref[0, 0, 0])
    strength = scal_ref[1]
    rgb = rgb_ref[...]
    mix = critic_ref[...]
    out = mix[:, 4:5]
    taps = [phase_taps(row_parity, col_parity, 1) for col_parity in (0, 1)]
    per_phase = PIX // TILE
    clear_pads(grad_ref, 0)
    clear_pads(grad_ref, 1)

    def convolve(index):
        start = (index % per_phase) * TILE
        raw = None
        for tap, phase, copy, first in taps[index // per_phase]:
            part = mul(tap_rows(map_ref, phase, copy, first, start, TILE), turned_ref[tap], NN)
            raw = part if raw is None else raw + part
        raw_buf[index % 3] = raw

    def judge(index):
        col_parity = index // per_phase
        start = (index % per_phase) * TILE
        raw = raw_buf[index % 3]
        noise = noise_all[start : start + TILE, col_parity : col_parity + 1]
        pre = raw * demod + (strength * noise + bias)
        half = half_tanh(pre)
        act = leaky(pre, half, ROOT_TWO)
        act_buf[index % 2] = act
        half_buf[index % 2] = half
        modulated = (act * style_three).astype(jnp.bfloat16)
        colors = jnp.transpose(mul(modulated, rgb_cols_ref[...], NN))[0:8]
        colors = colors + base_ref[0, :, start : start + TILE]
        hidden = mix[:, 3:4]
        for color in range(3):
            hidden = hidden + mix[:, color : color + 1] * colors[color : color + 1]
        hidden_half = half_tanh(hidden)
        logits = column_sums(out * leaky(hidden, hidden_half, 1.0))
        mask = mask_ref[0, 0, col_parity : col_parity + 1, start : start + TILE]
        grad_logits = -mask / (1.0 + jnp.exp(logits))
        grad_hidden = out * grad_logits * slope(hidden_half)
        grad_colors = jnp.concatenate(
            [column_sums(mix[:, color : color + 1] * grad_hidden) for color in range(3)]
            + [jnp.zeros((5, TILE), jnp.float32)],
            axis=0,
        )
        for lane in range(0, TILE, 128):
            color_ref[0] += grad_colors[:, lane : lane + 128]
        low_buf[index % 2] = jnp.concatenate(
            [grad_colors, jnp.zeros((8, TILE), jnp.float32)], axis=0
        ).astype(jnp.bfloat16)

    def finish(index):
        col_parity = index // per_phase
        start = (index % per_phase) * TILE
        raw = raw_buf[index % 3]
        act = act_buf[index % 2]
        half = half_buf[index % 2]
        grad_low = low_buf[index % 2]
        noise = noise_all[start : start + TILE, col_parity : col_parity + 1]
        modulated = (act * style_three).astype(jnp.bfloat16)
        grad_map = mul(grad_low, rgb, TN)
        grad_pre = grad_map * slope_of(style_three, half)
        write_map(grad_ref, col_parity, pl.ds(PAD + start, TILE), grad_pre * demod, col_parity == 1)
        add_rows(total_buf, 0, grad_map * act)
        add_rows(total_buf, 1, grad_pre * raw)
        add_rows(total_buf, 2, grad_pre)
        add_rows(total_buf, 3, grad_pre * noise)
        total_buf[4] += mul(grad_low, modulated, NN)[0:8]

    steps = 2 * per_phase
    for index in range(steps + 2):
        if index < steps:
            convolve(index)
        if 0 < index <= steps:
            judge(index - 1)
        if index > 1:
            finish(index - 2)

    @pl.when(row_parity == 1)
    def _():
        for row in range(4):
            sums_ref[0, row : row + 1, :] = column_sums(total_buf[row])
        sums_ref[0, 8:16, :] = total_buf[4]
        coef = -0.5 * demod * demod * demod * sums_ref[0, 1:2, :]
        sums_ref[0, 4:5, :] = coef
        back = exact(jnp.broadcast_to(coef, (8, coef.shape[1])), sq_buf[...], NN)[0:1]
        sums_ref[0, 5:6, :] = 2.0 * style_two * back

    @pl.when(last_step())
    def _():
        pltpu.make_async_copy(weight_ref, whole_ref, out_sem).wait()


def outer(lefts, rights):
    short = -len(lefts) % 8
    empty = [jnp.zeros((short, lefts[0].shape[1]), jnp.float32)] if short else []
    return exact(jnp.concatenate(lefts + empty), jnp.concatenate(rights + empty), TN)


def spread_out(me, order, layout, acc_ref, weight_ref, squares, out_refs):
    for tap in range(weight_ref.shape[0]):
        acc_ref[tap] += 2.0 * weight_ref[tap].astype(jnp.float32) * squares
    if layout is None:
        out_refs[0][0] = acc_ref[...].astype(out_refs[0].dtype)
        return
    for offsets, out_ref in zip(order, out_refs):
        for index, offset in enumerate(offsets):
            rows, cols = place_of(me ^ offset, layout)
            out_ref[index] = acc_ref[:, rows, cols].astype(out_ref.dtype)


def stacked_rows(rows, count):
    short = count - len(rows)
    empty = [jnp.zeros((short, rows[0].shape[1]), rows[0].dtype)] if short else []
    return jnp.concatenate(rows + empty)


def small_planes(me, layout, lat_ref, sums_one_ref, sums_ref, feat_sums_ref, color_ref, acc_ref):
    images = range(lat_ref.shape[0])
    _, rows, cols = layout
    chans = acc_ref.shape[2]
    style_rows = [
        [feat_sums_ref[image, 0:1, :] for image in images],
        [sums_one_ref[image, 0:1, :] + sums_ref[image, 5:6, :] for image in images],
        [sums_ref[image, 0:1, :] for image in images],
    ]
    latents = stacked_rows([lat_ref[image].astype(jnp.float32) for image in images], 16)
    latents = latents.astype(jnp.bfloat16)
    sums = []
    for number in range(3):
        grads = stacked_rows(style_rows[number], 16).astype(jnp.bfloat16)
        acc_ref[3 + number] = mul(latents, grads, TN)
        sums.append(column_sums(grads.astype(jnp.float32)))
    sums.append(sum(sums_one_ref[image, 2:3, :] for image in images))
    sums.append(sum(sums_ref[image, 2:3, :] for image in images))
    for color in range(3):
        row = 8 + color
        sums.append(sum(sums_ref[image, row : row + 1, :] for image in images) * C ** (-0.5))
    scalars = [
        sum(sums_one_ref[image, 3:4, :] for image in images),
        sum(sums_ref[image, 3:4, :] for image in images),
    ] + [sum(color_ref[image, color : color + 1, :] for image in images) for color in range(3)]
    lane = lax.broadcasted_iota(jnp.int32, (1, chans), 1) & (cols - 1)
    row = jnp.zeros((1, chans), jnp.float32)
    for number, values in enumerate(scalars):
        total = jnp.sum(values, axis=1, keepdims=True)
        row = jnp.where(lane == len(scalars) * me + number, total, row)
    pieces = []
    for _ in range(3):
        piece = row.astype(jnp.bfloat16).astype(jnp.float32)
        pieces.append(piece)
        row = row - piece
    block = jnp.concatenate([stacked_rows(sums, 16), stacked_rows(pieces, rows - 16)])
    for start in range(0, chans, rows):
        acc_ref[6, start : start + rows, :] = block


def flat_weight(order, layout, part, waits, *refs):
    me_ref, grad_ref, map_ref, weight_ref, vec_ref, sums_ref = refs[waits : waits + 6]
    token_ref, acc_ref = refs[-2:]
    small = acc_ref.shape[0] > 3
    small_refs = refs[waits + 6 : waits + 10] if small else ()
    out_refs = refs[waits + 6 + len(small_refs) : -2]
    row_parity = pl.program_id(1)
    first = pl.multiple_of(PAD * ((row_parity + part + 1) >> 1), PAD)

    @pl.when(first_step())
    def _():
        acc_ref[...] = jnp.zeros_like(acc_ref)

    for col_parity in (0, 1):
        grad = grad_ref[0, col_parity, 0, PAD : PAD + PIX, :]
        for tap in range(3):
            across_to = col_parity + tap + 1
            copy = 1 if across_to in (1, 4) else 0
            acc_ref[tap] += mul(grad, map_ref[0, across_to & 1, copy, pl.ds(first, PIX), :], TN)

    @pl.when(last_step())
    def _():
        images = range(vec_ref.shape[0])
        squares = outer(
            [sums_ref[image, 4:5, :] for image in images],
            [vec_ref[image, 1:2, :] * vec_ref[image, 1:2, :] for image in images],
        )
        if small:
            lat_ref, sums_one_ref, feat_sums_ref, color_ref = small_refs
            small_planes(
                me_ref[0], layout, lat_ref, sums_one_ref, sums_ref, feat_sums_ref, color_ref, acc_ref
            )
        spread_out(me_ref[0], order, layout, acc_ref, weight_ref, squares, out_refs)
        token_ref[...] = squares[0:8, 0:128]


def coef_of(vec_ref, sums_ref, image):
    demod = vec_ref[image, 5:6, :]
    return -0.5 * demod * demod * demod * sums_ref[image, 1:2, :]


def up_weight(order, layout, *refs):
    me_ref, grad_ref, xs_ref, weight_ref, vec_ref, sums_ref = refs[:6]
    out_refs, acc_ref = refs[6:-1], refs[-1]

    @pl.when(pl.program_id(0) == 0)
    def _():
        acc_ref[...] = jnp.zeros_like(acc_ref)

    for phase in range(4):
        grad = grad_ref[0, phase, 0, PAD:, :]
        for tap, col_step, row_step in UP_TAPS[phase]:
            acc_ref[tap] += mul(grad, xs_ref[0, col_step, pl.ds(PAD * row_step, PIX), :], TN)

    @pl.when(pl.program_id(0) == pl.num_programs(0) - 1)
    def _():
        images = range(vec_ref.shape[0])
        squares = outer(
            [coef_of(vec_ref, sums_ref, image) for image in images],
            [vec_ref[image, 0:1, :] * vec_ref[image, 0:1, :] for image in images],
        )
        spread_out(me_ref[0], order, layout, acc_ref, weight_ref, squares, out_refs)


def flat_back(
    scal_ref, grad_ref, raw_ref, vec_ref, noise_ref, weight_ref, out_ref, sums_ref, back_buf, total_buf
):
    row_parity = pl.program_id(1)

    @pl.when(row_parity == 0)
    def _():
        total_buf[...] = jnp.zeros_like(total_buf)

    style_two = vec_ref[0, 1:2, :]
    bias = vec_ref[0, 3:4, :]
    demod = vec_ref[0, 5:6, :]
    noise_all = jnp.transpose(noise_ref[0, 0, 0])
    strength = scal_ref[0]
    taps = [phase_taps(row_parity, col_parity, -1) for col_parity in (0, 1)]
    per_phase = PIX // TILE
    clear_pads(out_ref, 0, False)
    clear_pads(out_ref, 1, False)

    def convolve(index):
        start = (index % per_phase) * TILE
        total = None
        for tap, phase, copy, first in taps[index // per_phase]:
            part = mul(tap_rows(grad_ref, phase, copy, first, start, TILE), weight_ref[tap], NN)
            total = part if total is None else total + part
        back_buf[index % 2] = total

    def finish(index):
        col_parity = index // per_phase
        start = (index % per_phase) * TILE
        grad_map = back_buf[index % 2]
        raw = raw_ref[0, col_parity, pl.ds(start, TILE), :]
        noise = noise_all[start : start + TILE, col_parity : col_parity + 1]
        pre = raw * demod + (strength * noise + bias)
        half = half_tanh(pre)
        grad_pre = grad_map * slope_of(style_two, half)
        write_map(out_ref, col_parity, pl.ds(PAD + start, TILE), grad_pre * demod, col_parity == 1)
        add_rows(total_buf, 0, grad_map * leaky(pre, half, ROOT_TWO))
        add_rows(total_buf, 1, grad_pre * raw)
        add_rows(total_buf, 2, grad_pre)
        add_rows(total_buf, 3, grad_pre * noise)

    steps = 2 * per_phase
    for index in range(steps + 1):
        if index < steps:
            convolve(index)
        if index > 0:
            finish(index - 1)

    @pl.when(row_parity == 1)
    def _():
        for row in range(4):
            sums_ref[0, row : row + 1, :] = column_sums(total_buf[row])
        sums_ref[0, 4:8, :] = jnp.zeros((4, sums_ref.shape[2]), jnp.float32)


def up_back(layout, *refs):
    _, me_ref, grad_ref, feat_ref, vec_ref, sums_in_ref, sq_ref, weight_ref = refs[:8]
    sums_ref, turned_ref = refs[-2:]
    out_refs = refs[8:-2]
    style_one = vec_ref[0, 0:1, :]
    total = None
    for start in range(0, PIX, TILE):
        grad_map = None
        for phase in range(4):
            for tap, col_step, row_step in UP_TAPS[phase]:
                rows = grad_ref[0, phase, col_step, pl.ds(PAD + start - PAD * row_step, TILE), :]
                part = mul(rows, weight_ref[tap], NN)
                grad_map = part if grad_map is None else grad_map + part
        found = column_sums(grad_map * feat_ref[0, pl.ds(start, TILE), :].astype(jnp.float32))
        total = found if total is None else total + found
        turned = jnp.transpose(grad_map * style_one)
        here = pl.ds(start, TILE)
        if layout is None:
            out_refs[0][0, :, here] = turned
        else:
            turned_ref[...] = turned
            for offset, out_ref in zip((0, BIT_X), out_refs):
                _, cols = place_of(me_ref[0] ^ offset, layout)
                out_ref[0, :, here] = turned_ref[cols, :].astype(out_ref.dtype)
    coef = coef_of(vec_ref, sums_in_ref, 0)
    back = exact(jnp.broadcast_to(coef, (8, coef.shape[1])), sq_ref[...], NN)
    sums_ref[0] = total + 2.0 * style_one * back


def small_finish(gain, *refs):
    planes_ref, pick_ref = refs[:2]
    old_refs, new_refs = refs[2:17], refs[17:]

    def step(number, gradient, old=slice(None)):
        olds = [ref[old] for ref in old_refs[3 * number : 3 * number + 3]]
        found = adam_step(*olds, gradient, float(STEP))
        for ref, value in zip(new_refs[3 * number : 3 * number + 3], found):
            ref[old] = value

    for number in range(3):
        step(0, planes_ref[number] * gain, number)
    step(1, planes_ref[3, 0:3, :])
    step(2, planes_ref[3, 3:5, :])
    step(3, planes_ref[3, 5:8, :])
    row = planes_ref[3, 16:17, :] + planes_ref[3, 17:18, :] + planes_ref[3, 18:19, :]
    sums = exact(jnp.broadcast_to(row, (8, row.shape[1])), pick_ref[...], NN)
    step(4, sums[0:1, 0:5])


def call_small_finish(planes, olds, gain, devices):
    lanes = jnp.arange(planes.shape[2], dtype=jnp.int32)[:, None]
    pick = (lanes % 5 == jnp.arange(128, dtype=jnp.int32)) & (lanes < 5 * devices)
    olds = [old if old.ndim > 1 else old[None] for old in olds]
    out_shape = tuple(jax.ShapeDtypeStruct(old.shape, old.dtype) for old in olds)
    found = pl.pallas_call(
        functools.partial(small_finish, gain),
        in_specs=[pl.BlockSpec(memory_space=pltpu.VMEM)] * (2 + len(olds)),
        out_specs=[pl.BlockSpec(memory_space=pltpu.VMEM)] * len(olds),
        out_shape=out_shape,
        compiler_params=params(),
        name="small_finish",
    )(planes, pick.astype(jnp.float32), *olds)
    return tuple(found[:-3]) + tuple(value[0] for value in found[-3:])


def whole(shape):
    zeros = (0,) * len(shape)
    return pl.BlockSpec(shape, lambda *ids: zeros)


def per_image(shape):
    zeros = (0,) * (len(shape) - 1)
    return pl.BlockSpec((1,) + tuple(shape[1:]), lambda image, *ids: (image,) + zeros)


SMEM = pl.BlockSpec(memory_space=pltpu.SMEM)
ANY = pl.BlockSpec(memory_space=pl.ANY)


def cost(flops, moved):
    return pl.CostEstimate(flops=int(flops), bytes_accessed=int(moved), transcendentals=0)


def half_phases(shape, count=2):
    zeros = (0,) * (len(shape) - 2)
    return pl.BlockSpec(
        (1, count) + tuple(shape[2:]), lambda image, turn: (image, turn) + zeros
    )


def noise_spec(layer):
    return pl.BlockSpec((1, 1, 1, 8, PIX), lambda image, parity: (image, layer, parity, 0, 0))


def offsets_of(weight):
    return tuple(offsets for offsets, _ in weight[0])


def call_up_forward(after, me, scalars, feat, lat, small, noise, weight):
    images, _, chans = feat.shape
    arrays, layout = [array for _, array in weight[0]], weight[1]
    out_shape = (
        jax.ShapeDtypeStruct((images, 4, PIX, chans), jnp.float32),
        jax.ShapeDtypeStruct((images, 4, 2, ROWS, chans), jnp.bfloat16),
        jax.ShapeDtypeStruct((images, 2, PIX + PAD, chans), jnp.bfloat16),
        jax.ShapeDtypeStruct((chans, chans), jnp.float32),
        jax.ShapeDtypeStruct((images, 8, chans), jnp.float32),
        jax.ShapeDtypeStruct((9, chans, chans), jnp.bfloat16),
    )
    return pl.pallas_call(
        functools.partial(
            up_forward, offsets_of(weight), layout, lat.shape[2] ** (-0.5), len(after)
        ),
        grid=(images, 4),
        in_specs=[ANY] * len(after)
        + [
            SMEM,
            SMEM,
            per_image(feat.shape),
            per_image(lat.shape),
            whole(small.shape),
            pl.BlockSpec((1, 1, 2, 8, PIX), lambda image, turn: (image, 0, 0, 0, 0)),
        ]
        + [ANY] * len(arrays),
        out_specs=[
            half_phases(out_shape[0].shape, 1),
            half_phases(out_shape[1].shape, 1),
            per_image(out_shape[2].shape),
            whole(out_shape[3].shape),
            per_image(out_shape[4].shape),
            ANY,
        ],
        out_shape=out_shape,
        scratch_shapes=[
            pltpu.VMEM((2, TILE, chans), jnp.float32),
            pltpu.VMEM((12, chans, chans), jnp.bfloat16),
            pltpu.SemaphoreType.DMA((sum(len(o) for o in offsets_of(weight)),)),
            pltpu.SemaphoreType.DMA,
        ],
        compiler_params=params(),
        cost_estimate=cost(18 * images * PIX * chans * chans, 60e6),
        name="up_forward",
    )(*after, me, scalars, feat, lat, small, noise, *arrays)


def call_flat_forward(me, scalars, maps, vecs, noise, base, mask, critic, rgb, weight):
    images, chans = maps.shape[0], maps.shape[-1]
    arrays, layout = [array for _, array in weight[0]], weight[1]
    rgb_cols = jnp.concatenate([jnp.transpose(rgb), jnp.zeros((chans, 112), rgb.dtype)], axis=1)
    out_shape = (
        jax.ShapeDtypeStruct((images, 4, 2, ROWS, chans), jnp.bfloat16),
        jax.ShapeDtypeStruct((images, 16, chans), jnp.float32),
        jax.ShapeDtypeStruct((images, 8, 128), jnp.float32),
        jax.ShapeDtypeStruct((9, chans, chans), jnp.bfloat16),
    )
    return pl.pallas_call(
        functools.partial(flat_forward, offsets_of(weight), layout),
        grid=(images, 2),
        in_specs=[
            SMEM,
            SMEM,
            per_image(maps.shape),
            per_image(vecs.shape),
            noise_spec(1),
            per_image(base.shape),
            pl.BlockSpec((1, 1, 8, PIX), lambda image, parity: (image, parity, 0, 0)),
            whole(critic.shape),
            whole(rgb.shape),
            whole(rgb_cols.shape),
        ]
        + [ANY] * len(arrays),
        out_specs=[
            half_phases(out_shape[0].shape),
            per_image(out_shape[1].shape),
            per_image(out_shape[2].shape),
            ANY,
        ],
        out_shape=out_shape,
        scratch_shapes=[
            pltpu.VMEM((3, TILE, chans), jnp.float32),
            pltpu.VMEM((2, TILE, chans), jnp.float32),
            pltpu.VMEM((2, TILE, chans), jnp.float32),
            pltpu.VMEM((2, 16, TILE), jnp.bfloat16),
            pltpu.VMEM((9, chans, chans), jnp.bfloat16),
            pltpu.VMEM((chans, chans), jnp.float32),
            pltpu.VMEM((5, 8, chans), jnp.float32),
            pltpu.VMEM((9, chans, chans), jnp.bfloat16),
            pltpu.SemaphoreType.DMA((sum(len(o) for o in offsets_of(weight)),)),
            pltpu.SemaphoreType.DMA,
        ],
        compiler_params=params(),
        cost_estimate=cost(72 * images * PIX * chans * chans, 60e6),
        name="flat_forward",
    )(me, scalars, maps, vecs, noise, base, mask, critic, rgb, rgb_cols, *arrays)


def gradient_shapes(chans, taps, layout):
    if layout is None:
        return (jax.ShapeDtypeStruct((1, taps, chans, chans), jnp.float32),)
    _, rows, cols = layout
    shape = (16, taps, rows, cols)
    return (jax.ShapeDtypeStruct(shape, jnp.float32), jax.ShapeDtypeStruct(shape, jnp.bfloat16))


def call_flat_weight(me, after, grad, maps, weight, vecs, sums, order, layout, part, small=()):
    images, chans = maps.shape[0], maps.shape[-1]
    planes = 7 if small else 3
    out_shape = gradient_shapes(chans, planes, layout) + (jax.ShapeDtypeStruct((8, 128), jnp.float32),)
    return pl.pallas_call(
        functools.partial(flat_weight, order, layout, part, len(after)),
        grid=(images, 2),
        in_specs=[ANY] * len(after)
        + [
            SMEM,
            pl.BlockSpec((1, 2, 1, ROWS, chans), lambda image, parity: (image, parity, 0, 0, 0)),
            pl.BlockSpec(
                (1, 2, 2, ROWS, chans), lambda image, parity: (image, (parity + part + 1) & 1, 0, 0, 0)
            ),
            pl.BlockSpec((3, chans, chans), lambda image, parity: (part, 0, 0)),
            whole(vecs.shape),
            whole(sums.shape),
        ]
        + [whole(array.shape) for array in small],
        out_specs=[whole(s.shape) for s in out_shape],
        out_shape=out_shape,
        scratch_shapes=[pltpu.VMEM((planes, chans, chans), jnp.float32)],
        compiler_params=params(),
        cost_estimate=cost(24 * images * PIX * chans * chans, 40e6),
        name="flat_weight_" + str(part),
    )(*after, me, grad, maps, weight, vecs, sums, *small)


def call_flat_back(scalars, grad, raw, vecs, noise, weight):
    images, chans = grad.shape[0], grad.shape[-1]
    out_shape = (
        jax.ShapeDtypeStruct((images, 4, 2, PIX + PAD, chans), jnp.bfloat16),
        jax.ShapeDtypeStruct((images, 8, chans), jnp.float32),
    )
    return pl.pallas_call(
        flat_back,
        grid=(images, 2),
        in_specs=[
            SMEM,
            per_image(grad.shape),
            half_phases(raw.shape),
            per_image(vecs.shape),
            noise_spec(0),
            whole(weight.shape),
        ],
        out_specs=[half_phases(out_shape[0].shape), per_image(out_shape[1].shape)],
        out_shape=out_shape,
        scratch_shapes=[
            pltpu.VMEM((2, TILE, chans), jnp.float32),
            pltpu.VMEM((4, 8, chans), jnp.float32),
        ],
        compiler_params=params(),
        cost_estimate=cost(72 * images * PIX * chans * chans, 60e6),
        name="flat_back",
    )(scalars, grad, raw, vecs, noise, weight)


def call_up_weight(me, grad, xs, weight, vecs, sums, order, layout):
    images, chans = xs.shape[0], xs.shape[-1]
    out_shape = gradient_shapes(chans, 9, layout)
    return pl.pallas_call(
        functools.partial(up_weight, order, layout),
        grid=(images,),
        in_specs=[
            SMEM,
            pl.BlockSpec((1, 4, 1, PIX + PAD, chans), lambda image: (image, 0, 0, 0, 0)),
            per_image(xs.shape),
            whole(weight.shape),
            whole(vecs.shape),
            whole(sums.shape),
        ],
        out_specs=[whole(s.shape) for s in out_shape],
        out_shape=out_shape,
        scratch_shapes=[pltpu.VMEM((9, chans, chans), jnp.float32)],
        compiler_params=params(),
        cost_estimate=cost(18 * images * PIX * chans * chans, 30e6),
        name="up_weight",
    )(me, grad, xs, weight, vecs, sums)


def call_up_back(after, me, grad, feat, vecs, sums, squares, weight, layout):
    images, _, chans = feat.shape
    if layout is None:
        out_shape = (jax.ShapeDtypeStruct((images, chans, PIX), jnp.float32),)
    else:
        shape = (images, layout[2], PIX)
        out_shape = (
            jax.ShapeDtypeStruct(shape, jnp.float32), jax.ShapeDtypeStruct(shape, jnp.bfloat16)
        )
    out_shape += (jax.ShapeDtypeStruct((images, 8, chans), jnp.float32),)
    return pl.pallas_call(
        functools.partial(up_back, layout),
        grid=(images,),
        in_specs=[
            ANY,
            SMEM,
            per_image(grad.shape),
            per_image(feat.shape),
            per_image(vecs.shape),
            per_image(sums.shape),
            whole(squares.shape),
            whole(weight.shape),
        ],
        out_specs=[per_image(s.shape) for s in out_shape],
        out_shape=out_shape,
        scratch_shapes=[pltpu.VMEM((chans, TILE), jnp.float32)],
        compiler_params=params(),
        cost_estimate=cost(18 * images * PIX * chans * chans, 30e6),
        name="up_back",
    )(after, me, grad, feat, vecs, sums, squares, weight)


BIT_X, BIT_CORE, BIT_Y, BIT_LOW, BIT_HIGH = 1, 2, 4, 8, 16
Z_OFFSETS = ((0, BIT_LOW), (BIT_HIGH, BIT_HIGH + BIT_LOW))


def across(values, bits, devices):
    return lax.ppermute(values, BOTH, [(device, device ^ bits) for device in range(devices)])


def gather_along_z(block, devices):
    move = lambda values, bits: across(values, bits, devices)
    low = jnp.stack([block, move(block, BIT_LOW)])
    return low, jnp.stack([move(block, BIT_HIGH), move(block, BIT_HIGH + BIT_LOW)])


def gather_in_turn(low, high, devices, beside):
    move = lambda values, bits: across(values, bits, devices)
    high_y, low_y = move(high, BIT_Y), move(low, BIT_Y)
    low_x, high_x = move(low, BIT_X), move(high, BIT_X)
    (low_x, high_y), beside = lax.optimization_barrier(((low_x, high_y), beside))
    low_xy, high_xy = move(low_x, BIT_Y), move(high_y, BIT_X)
    found = []
    for offsets, arrays in zip(
        Z_OFFSETS, ((low, low_x, low_y, low_xy), (high, high_x, high_y, high_xy))
    ):
        for bits, array in zip((0, BIT_X, BIT_Y, BIT_X + BIT_Y), arrays):
            found.append((tuple(o ^ bits for o in offsets), array))
    return found, beside


def gather_at_once(along, devices):
    found = []
    offsets = Z_OFFSETS[0] + Z_OFFSETS[1]
    for bits in (0, BIT_X + BIT_Y, BIT_X, BIT_Y):
        array = across(along, bits, devices) if bits else along
        found.append((tuple(o ^ bits for o in offsets), array))
    return found


def with_other_core(found, devices):
    return found + [
        (tuple(o ^ BIT_CORE for o in offsets), across(array, BIT_CORE, devices))
        for offsets, array in found
    ]


def tie(values, token):
    return values if token is None else lax.optimization_barrier((values, token))[0]


PLANE_OFFSETS = (BIT_X, BIT_Y, BIT_X + BIT_Y)
Z_ALL = Z_OFFSETS[0] + Z_OFFSETS[1]


def scatter_order(at_once):
    if at_once:
        kept = [plane + z for plane in (0,) + PLANE_OFFSETS for z in Z_ALL]
    else:
        kept = []
        for high in (0, 1):
            one, two = (BIT_X, BIT_Y) if high == 0 else (BIT_Y, BIT_X)
            for a in (0, 1):
                for b in (0, 1):
                    kept += [z + a * one + b * two for z in Z_OFFSETS[high]]
    return tuple(kept), tuple(offset ^ BIT_CORE for offset in kept)


def scatter_blocks(kept, sent, devices, at_once):
    low = lambda values: values.astype(jnp.bfloat16)

    def swap(values, bits, token):
        found = tie([across(v, b, devices) for v, b in zip(values, bits)], token)
        return [f.astype(jnp.float32) for f in found]

    token = yield (sent,)
    total = kept + swap((sent,), (BIT_CORE,), token)[0]
    if at_once:
        total = total.reshape((4, 4) + kept.shape[1:])
        sends = low(total[1]), low(total[2]), low(total[3])
        token = yield sends
        mine = total[0]
        for found in swap(sends, PLANE_OFFSETS, token):
            mine = mine + found
        mine = [mine[0], mine[1], mine[2], mine[3]]
    else:
        total = total.reshape((2, 2, 2, 2) + kept.shape[1:])
        sends = low(total[0, 1]), low(total[1, 1])
        token = yield sends
        found = swap(sends, (BIT_X, BIT_Y), token)
        halves = total[0, 0] + found[0], total[1, 0] + found[1]
        sends = low(halves[0][1]), low(halves[1][1])
        token = yield sends
        found = swap(sends, (BIT_Y, BIT_X), token)
        halves = halves[0][0] + found[0], halves[1][0] + found[1]
        mine = [halves[0][0], halves[0][1], halves[1][0], halves[1][1]]
    sends = low(mine[1]), low(mine[2]), low(mine[3])
    token = yield sends
    total = mine[0]
    for found in swap(sends, Z_ALL[1:], token):
        total = total + found
    yield total


def gather_whole(block, n_img, n_ch):
    _, rows, cols = block.shape
    every = lax.all_gather(block, BOTH, axis=0, tiled=False)
    every = every.reshape(n_img, n_ch, -1, rows, cols)
    return jnp.transpose(every, (2, 0, 3, 1, 4)).reshape(-1, n_img * rows, n_ch * cols)


def scatter_whole(grad, n_img, n_ch, rows, cols):
    grad = grad.reshape(-1, n_img, rows, n_ch, cols)
    grad = jnp.transpose(grad, (1, 3, 0, 2, 4)).reshape(n_img * n_ch, -1, rows, cols)
    return lax.psum_scatter(grad, BOTH, scatter_dimension=0, tiled=False)


def adam_step(weight, mean_old, square_old, gradient, count):
    moment = BETA_ONE * mean_old + (1.0 - BETA_ONE) * gradient
    variance = BETA_TWO * square_old + (1.0 - BETA_TWO) * gradient * gradient
    fix_one = 1.0 - BETA_ONE**count
    fix_two = 1.0 - BETA_TWO**count
    update = moment / fix_one / (jnp.sqrt(variance / fix_two) + ADAM_EPS) + DECAY_RATE * weight
    return (weight - LEARN_RATE * update, moment, variance)


def phases_of_lanes(side):
    column = jnp.arange(side, dtype=jnp.int32)
    target = (column % 2) * (side // 2) + column // 2
    return (target[:, None] == column[None, :]).astype(jnp.float32)


def padded(values, rows):
    short = rows - values.shape[-2]
    shape = values.shape[:-2] + (short, values.shape[-1])
    return jnp.concatenate([values, jnp.zeros(shape, values.dtype)], axis=-2)


def body(
    n_img,
    n_ch,
    features,
    latents,
    skip_rgb,
    noises,
    ada_shift,
    crop_mask,
    critic_mix,
    critic_bias,
    critic_out,
    upsampler,
    upsampler_mean,
    upsampler_square,
    refiner,
    refiner_mean,
    refiner_square,
    affines,
    affines_mean,
    affines_square,
    modbias,
    modbias_mean,
    modbias_square,
    actbias,
    actbias_mean,
    actbias_square,
    rgbmix,
    rgbmix_mean,
    rgbmix_square,
    scalars,
    scalars_mean,
    scalars_square,
):
    local_chans, group_images = features.shape[0], features.shape[1]
    chans = local_chans * n_ch
    rows_own = upsampler.shape[2]
    side = 2 * RES
    devices = n_img * n_ch
    by_hand = devices == 32 and n_ch == 2 and group_images % n_ch == 0
    share = max(1, n_ch // group_images)
    images = group_images * share // n_ch
    ch_index = lax.axis_index("ch")
    img_index = lax.axis_index("img")
    me = (img_index * n_ch + ch_index).astype(jnp.int32)[None]
    first = (ch_index // share) * images
    col_start = ch_index * local_chans

    def mine(values, axis):
        return lax.dynamic_slice_in_dim(values, first, images, axis)

    def my_chans(values, axis):
        return lax.dynamic_slice_in_dim(values, col_start, local_chans, axis)

    up_block = jnp.concatenate([jnp.transpose(upsampler, (1, 2, 0)), affines]).astype(jnp.bfloat16)
    ref_block = jnp.transpose(refiner, (1, 2, 0)).astype(jnp.bfloat16)
    small_own = jnp.concatenate([modbias, actbias, rgbmix], axis=0)
    if by_hand:
        layout = (n_ch, rows_own, local_chans)
        other = lax.dynamic_slice_in_dim(features, images - first, images, 1)
        other = across(other, BIT_X, devices)
        up_low, up_high = gather_along_z(up_block, devices)
        ref_along = jnp.concatenate(gather_along_z(ref_block, devices))
        here = mine(features, 1)
        feat = jnp.where(
            ch_index == 0, jnp.concatenate([here, other]), jnp.concatenate([other, here])
        )
        small_other = across(small_own, BIT_X, devices)
        small = jnp.where(
            ch_index == 0,
            jnp.concatenate([small_own, small_other], axis=1),
            jnp.concatenate([small_other, small_own], axis=1),
        )
    else:
        layout, ahead = None, ()
        up_weight_all = ([((0,), gather_whole(up_block, n_img, n_ch))], None)
        ref_weight_all = ([((0,), gather_whole(ref_block, n_img, n_ch))], None)
        small = lax.all_gather(small_own, "ch", axis=1, tiled=True)
        feat = mine(lax.all_gather(features, "ch", axis=0, tiled=True), 1)
    feat = jnp.transpose(feat, (1, 2, 0))
    lat_own = mine(latents, 0)
    rgb_low = padded(small[5:8] * C ** (-0.5), 16).astype(jnp.bfloat16)
    noise = jnp.dot(
        mine(noises, 1).reshape(2 * images * side, side), phases_of_lanes(side), precision=PRECISE
    )
    noise = jnp.transpose(noise.reshape(2, images, RES, 2, 2, RES), (1, 0, 3, 4, 2, 5))
    noise = padded(noise.reshape(images, 2, 2, 2, PIX), 8)
    order_in = jnp.arange(side, dtype=jnp.int32)
    order_in = 2 * (order_in % RES) + order_in // RES
    shifts = mine(ada_shift, 0)
    picks = [
        (((order_in[None, :] + shifts[:, axis : axis + 1]) % side)[:, :, None] == jnp.arange(side)).astype(
            jnp.bfloat16
        )
        for axis in (0, 1)
    ]
    mask = mine(crop_mask, 0).reshape(images, side, side).astype(jnp.bfloat16)
    mask = jnp.einsum("byz,bzx->byx", picks[0], mask, preferred_element_type=jnp.bfloat16)
    mask = jnp.einsum("byx,bwx->byw", mask, picks[1], preferred_element_type=jnp.float32) / share
    mask = jnp.transpose(mask.reshape(images, 2, RES, 2, RES), (0, 1, 3, 2, 4))
    mask = padded(mask.reshape(images, 2, 2, PIX), 8)
    base = padded(
        jnp.transpose(mine(skip_rgb, 1), (1, 0, 2)) + scalars[2:5][None, :, None], 8
    )
    critic = jnp.concatenate(
        [critic_mix, critic_bias[:, None], critic_out[:, None], jnp.zeros((critic_mix.shape[0], 3))], axis=1
    )
    if by_hand:
        beside = (feat, small, noise, mask, base, critic, rgb_low, ref_along)
        found, beside = gather_in_turn(up_low, up_high, devices, beside)
        feat, small, noise, mask, base, critic, rgb_low, ref_along = beside
        up_weight_all = (with_other_core(found, devices), layout)
        ref_plane = gather_at_once(ref_along, devices)
        ahead = (ref_along,)

    raw_one, maps, xs, up_square, vecs, up_full = call_up_forward(
        ahead, me, scalars, feat, lat_own[:, None, :], small, noise, up_weight_all
    )
    if by_hand:
        arrays, _ = lax.optimization_barrier(([array for _, array in ref_plane], vecs))
        ref_plane = [(offsets, array) for (offsets, _), array in zip(ref_plane, arrays)]
        ref_weight_all = (with_other_core(ref_plane, devices), layout)
    grad_two, sums_two, color_sums, ref_full = call_flat_forward(
        me, scalars, maps, vecs, noise, base, mask, critic, rgb_low, ref_weight_all
    )
    grad_one, sums_one = call_flat_back(scalars, grad_two, raw_one, vecs, noise, ref_full)
    up_parts = call_up_weight(
        me, grad_one, xs, up_full, vecs, sums_one, scatter_order(False), layout
    )
    *feat_grads, feat_sums = call_up_back(
        up_parts[0], me, grad_one, feat, vecs, sums_one, up_square, up_full, layout
    )

    def ref_part(after, part, at_once=False, small=()):
        return call_flat_weight(
            me,
            after,
            grad_two,
            maps,
            ref_full,
            vecs,
            sums_two,
            scatter_order(at_once),
            layout,
            part,
            small,
        )

    if by_hand:
        kept_grad, other = feat_grads
        small_sums = (lat_own[:, None, :], sums_one, feat_sums, color_sums)
        up_steps = scatter_blocks(*up_parts, devices, False)
        next(up_steps)
        kept, sent, token = ref_part(up_steps.send(feat_sums) + (other,), 0, small=small_sums)
        other = across(other, BIT_X, devices)
        first_steps = scatter_blocks(kept, sent, devices, False)
        next(first_steps)
        kept, sent, token = ref_part(up_steps.send(token) + (token,), 1, True)
        steps = [scatter_blocks(kept, sent, devices, True)]
        next(steps[0])
        kept, sent, token = ref_part(
            up_steps.send(token) + first_steps.send(token) + (token,), 2, True
        )
        steps.append(scatter_blocks(kept, sent, devices, True))
        next(steps[1])
        last = steps[1].send(None)
        first_steps.send(token)
        steps[0].send(token)
        first_steps.send(last)
        steps[0].send(last)
        up_grad = up_steps.send(last)
        last = steps[1].send(None)
        other = tie(other, last)
        first_grad, next_grad = first_steps.send(last), steps[0].send(last)
        ref_grad = jnp.concatenate([first_grad[0:3], next_grad, steps[1].send(None)])
    else:
        up_grad = scatter_whole(up_parts[0], n_img, n_ch, rows_own, local_chans)
        ref_grad = jnp.concatenate(
            [
                scatter_whole(ref_part((), part)[0], n_img, n_ch, rows_own, local_chans)
                for part in range(3)
            ]
        )
    up_grad = jnp.transpose(up_grad, (2, 0, 1))
    ref_grad = jnp.transpose(ref_grad, (2, 0, 1))

    if by_hand:
        other = other.astype(jnp.float32)
        feat_grad = jnp.where(
            ch_index == 0, jnp.concatenate([kept_grad, other]), jnp.concatenate([other, kept_grad])
        )
    else:
        feat_grad = lax.all_gather(feat_grads[0], "ch", axis=0, tiled=True)[::share] * share
        feat_grad = my_chans(feat_grad, 1)
    features_grad = jnp.transpose(feat_grad, (1, 0, 2))

    count = float(STEP)
    style_gain = latents.shape[1] ** (-0.5)
    small_old = (
        affines,
        affines_mean,
        affines_square,
        modbias,
        modbias_mean,
        modbias_square,
        actbias,
        actbias_mean,
        actbias_square,
        rgbmix,
        rgbmix_mean,
        rgbmix_square,
        scalars,
        scalars_mean,
        scalars_square,
    )
    if by_hand:
        small_new = call_small_finish(first_grad[3:7], small_old, style_gain, devices)
    else:
        style_grads = jnp.stack(
            [feat_sums[:, 0], sums_one[:, 0] + sums_two[:, 5], sums_two[:, 0]]
        )
        style_grads = style_grads.astype(jnp.bfloat16).astype(jnp.float32)
        color_sum = jnp.sum(color_sums[:, 0:3], axis=(0, 2))
        scalar_row = jnp.concatenate(
            [
                jnp.sum(sums_one[:, 3])[None],
                jnp.sum(sums_two[:, 3])[None],
                color_sum,
                jnp.zeros((chans - 5,), jnp.float32),
            ]
        )
        packed = jnp.concatenate(
            [
                style_grads.reshape(3 * images, chans),
                lat_own.astype(jnp.float32),
                jnp.sum(sums_one[:, 2], axis=0)[None],
                jnp.sum(sums_two[:, 2], axis=0)[None],
                jnp.sum(sums_two[:, 8:11], axis=0) * C ** (-0.5),
                scalar_row[None],
            ],
            axis=0,
        )
        packed = padded(packed, 16)
        every = lax.all_gather(packed, BOTH, axis=0, tiled=False)
        first_sum = 4 * images
        sums = jnp.sum(every[:, first_sum : first_sum + 6], axis=0)
        lat_rows = affines.shape[1]
        lat_cols = every[:, 3 * images : first_sum]
        lat_cols = lax.dynamic_slice_in_dim(lat_cols, img_index * lat_rows, lat_rows, 2)
        style_all = my_chans(every[:, : 3 * images], 2)
        style_all = style_all.reshape(devices, 3, images, local_chans)
        aff_grad = style_gain * jnp.einsum(
            "dbj,dkbi->kji",
            lat_cols.astype(jnp.bfloat16),
            style_all.astype(jnp.bfloat16),
            preferred_element_type=jnp.float32,
        )
        small_grad = my_chans(sums[0:5], 1)
        small_new = ()
        for number, gradient in enumerate(
            (aff_grad, jnp.sum(style_all, axis=(0, 2)), small_grad[0:2], small_grad[2:5], sums[5, 0:5])
        ):
            small_new += adam_step(*small_old[3 * number : 3 * number + 3], gradient, count)

    up_new = adam_step(upsampler, upsampler_mean, upsampler_square, up_grad, count)
    ref_new = adam_step(refiner, refiner_mean, refiner_square, ref_grad, count)
    return (features_grad,) + up_new + ref_new + tuple(small_new)


def solution(mesh):
    conv = P("ch", None, "img")
    aff = P(None, "img", "ch")
    row = P(None, "ch")
    images = P(None, "img", None)
    return jax.shard_map(
        functools.partial(body, mesh.shape["img"], mesh.shape["ch"]),
        mesh=mesh,
        in_specs=(P("ch", "img", None), P("img", None), images, images, P("img", None), P("img", None))
        + (P(),) * 3
        + (conv,) * 6
        + (aff,) * 3
        + (row,) * 9
        + (P(),) * 3,
        out_specs=(P("ch", "img", None),) + (conv,) * 6 + (aff,) * 3 + (row,) * 9 + (P(),) * 3,
        check_vma=False,
    )
```
